256 devices in a mesh: img: 16 (over z, x_lo), txt: 16 (over y, x_hi, core).
Axes of the slice: x: 4 (x_hi: 2, x_lo: 2; x = x_hi * 2 + x_lo), y: 4, z: 8, core: 2. Of those that a mesh axis runs over, the one named last changes fastest.
Arguments:
- image_hidden: bfloat16 [8192, 1152], P(('img', 'txt')), may hold values from -12 to 12
- image_acts: bfloat16 [8192, 4304], P('img', 'txt'), may hold values from -6 to 6
- image_proj: bfloat16 [4304, 1152], P('txt'), may hold values from -0.09375 to 0.09375
- text_hidden: bfloat16 [8192, 1152], P(('txt', 'img')), may hold values from -12 to 12
- text_acts: bfloat16 [8192, 4304], P('txt', 'img'), may hold values from -6 to 6
- text_proj: bfloat16 [4304, 1152], P('img'), may hold values from -0.09375 to 0.09375
- positives: int32 [8192], P('img'), may hold values from 0 to 8191, each once
- log_scale: float32 [1], replicated, may hold values from 1.6 to 2.7
- bias: float32 [1], replicated, may hold values from -7 to -5
Outputs:
- loss: float32 [1], replicated
- image_grad: bfloat16 [8192, 1152], P(('img', 'txt'))
- text_grad: bfloat16 [8192, 1152], P(('txt', 'img'))
- image_act_grad: bfloat16 [8192, 4304], P('img', 'txt')
- text_act_grad: bfloat16 [8192, 4304], P('txt', 'img')
- image_proj_grad: float32 [4304, 1152], P('txt', 'img')
- text_proj_grad: float32 [4304, 1152], P('img', 'txt')
The draws below stay inside these ranges and needn't reach their ends.
Inputs may be any that keep to these rules, and one draw needn't show every extreme that they name: `positives`: every text index is the positive of exactly one image.
All inputs are finite; a program needn't handle non-finite values.
Results may differ from the reference program's by a relative error of at most 0.007.
Values may be sent and summed in bfloat16 or wider, within the bound.
No kernel may reach another device: no remote copies, remote signals or barrier semaphores. Data moves between devices by JAX's collectives and lax.ppermute only.
A program may use at most 64 MiB of HBM per device.

```python
import jax
import jax.numpy as jnp
from jax import lax

D = 1152
FF = 4304
BATCH = 8192
N_IMG = 16


def common_direction(key):
    return jnp.clip(jax.random.normal(key, (D,), jnp.float32), -4.0, 4.0)


def ramped_rows(key, shared, amplitude, power):
    noise = jnp.clip(jax.random.normal(key, (BATCH, D), jnp.float32), -4.0, 4.0)
    ramp = amplitude * (jnp.arange(BATCH, dtype=jnp.float32) / (BATCH - 1)) ** power
    return jnp.clip(noise + ramp[:, None] * shared[None, :], -12.0, 12.0)


def draw_image_hidden(key, part):
    shared = common_direction(key)
    key = jax.random.fold_in(key, 11)
    values = ramped_rows(key, shared, 1.4, 1.0)
    return values.astype(jnp.bfloat16)


def draw_text_hidden(key, part):
    shared = common_direction(key)
    key = jax.random.fold_in(key, 23)
    values = ramped_rows(key, shared, 1.4, 1.0)
    return values.astype(jnp.bfloat16)


def block_levels(rng, shape, shards, least, high):
    gain = 1.0
    for position, shards_of in shards:
        steps = jax.random.uniform(jax.random.fold_in(jax.random.fold_in(rng, 6), position), (shards_of,), jnp.float32, least / len(shards), high / len(shards))
        gain = gain * jnp.repeat(jnp.exp(steps), shape[position] // shards_of).reshape((-1,) + (1,) * (len(shape) - 1 - position))
    return gain


def gaussian(own_key, shape, scale, reach, cuts=(), kind=jnp.bfloat16):
    array = scale * jax.random.normal(own_key, shape, jnp.float32)
    if cuts:
        array = array * block_levels(own_key, shape, cuts, -0.22, 0.18)
    return jnp.clip(array, -reach, reach).astype(kind)


def setup_inputs(seed: int = 0) -> dict:
    key_of = jax.random.split(jax.random.key(seed), 10)
    return {
        "image_hidden": draw_image_hidden(jax.random.fold_in(key_of[9], 71), 0),
        "image_acts": gaussian(key_of[1], (BATCH, FF), 1.0, 6.0, ((0, 16), (1, 16))),
        "image_proj": gaussian(key_of[2], (FF, D), FF ** -0.5, 0.09375, ((0, 16),)),
        "text_hidden": draw_text_hidden(jax.random.fold_in(key_of[9], 71), 0),
        "text_acts": gaussian(key_of[4], (BATCH, FF), 1.0, 6.0, ((0, 16), (1, 16))),
        "text_proj": gaussian(key_of[5], (FF, D), FF ** -0.5, 0.09375, ((0, 16),)),
        "positives": jax.random.permutation(key_of[6], BATCH).astype(jnp.int32),
        "log_scale": jnp.clip(jax.random.uniform(key_of[7], (1,), jnp.float32, 1.6, 2.7), 1.6, 2.7),
        "bias": jnp.clip(jax.random.uniform(key_of[8], (1,), jnp.float32, -7.0, -5.0), -7.0, -5.0),
    }


def normalize(embed):
    values = embed.astype(jnp.float32)
    inverse = lax.rsqrt(lax.optimization_barrier(jnp.sum(values * values, axis=-1, keepdims=True)) + 1e-06)
    return (values * inverse, inverse)

def norm_backward(embed, upstream):
    unit, inverse = normalize(embed)
    return inverse * (upstream - unit * lax.optimization_barrier(jnp.sum(unit * upstream, axis=-1, keepdims=True)))

def reference(image_hidden, image_acts, image_proj, text_hidden, text_acts, text_proj, positives, log_scale, bias):
    image_embed = (image_hidden.astype(jnp.float32) + jnp.dot(image_acts, image_proj, preferred_element_type=jnp.float32)).astype(jnp.bfloat16)
    text_embed = (text_hidden.astype(jnp.float32) + jnp.dot(text_acts, text_proj, preferred_element_type=jnp.float32)).astype(jnp.bfloat16)
    image_unit = normalize(image_embed)[0].astype(jnp.bfloat16)
    text_unit = normalize(text_embed)[0].astype(jnp.bfloat16)
    scale = jnp.exp(log_scale[0])
    block = BATCH // N_IMG
    columns = jnp.arange(BATCH, dtype=jnp.int32)[None, :]

    def step(carry, inputs):
        text_dir, total = carry
        image_rows, labels = inputs
        scores = scale * jnp.dot(image_rows, text_unit.T, preferred_element_type=jnp.float32) + bias[0]
        target = (labels[:, None] == columns).astype(jnp.float32)
        total = total + jnp.sum(jax.nn.softplus((1.0 - 2.0 * target) * scores))
        slope = (jax.nn.sigmoid(scores) - target).astype(jnp.bfloat16)
        image_dir = scale * jnp.dot(slope, text_unit, preferred_element_type=jnp.float32)
        text_dir = text_dir + scale * jnp.dot(slope.T, image_rows, preferred_element_type=jnp.float32)
        return ((text_dir, total), image_dir)
    start = (jnp.zeros((BATCH, D), jnp.float32), jnp.zeros((), jnp.float32))
    (text_dir, total), image_dirs = lax.scan(step, start, (image_unit.reshape(N_IMG, block, D), positives.reshape(N_IMG, block)))
    image_dir = image_dirs.reshape(BATCH, D)
    image_grad = norm_backward(image_embed, image_dir).astype(jnp.bfloat16)
    text_grad = norm_backward(text_embed, text_dir).astype(jnp.bfloat16)
    image_act_grad = jnp.dot(image_grad, image_proj.T, preferred_element_type=jnp.float32).astype(jnp.bfloat16)
    text_act_grad = jnp.dot(text_grad, text_proj.T, preferred_element_type=jnp.float32).astype(jnp.bfloat16)
    image_proj_grad = jnp.dot(image_acts.T, image_grad, preferred_element_type=jnp.float32)
    text_proj_grad = jnp.dot(text_acts.T, text_grad, preferred_element_type=jnp.float32)
    loss = jnp.reshape(total / BATCH, (1,))
    return (loss, image_grad, text_grad, image_act_grad, text_act_grad, image_proj_grad, text_proj_grad)
```

```python
import jax
import jax.numpy as jnp
from jax import lax
from jax.sharding import PartitionSpec as P


def normalize(embed):
    values = embed.astype(jnp.float32)
    inverse = lax.rsqrt(jnp.sum(values * values, axis=-1, keepdims=True) + 1e-06)
    return (values * inverse, inverse)


def contract_rows(left, right):
    return lax.dot_general(
        left, right, (((0,), (0,)), ((), ())), preferred_element_type=jnp.float32
    )


def contract_cols(left, right):
    return lax.dot_general(
        left, right, (((1,), (1,)), ((), ())), preferred_element_type=jnp.float32
    )


def scatter_sum(parts, axis):
    count = lax.axis_size(axis)
    blocks = parts.astype(jnp.bfloat16).reshape((count, -1) + parts.shape[1:])
    return jnp.sum(lax.all_to_all(blocks, axis, 0, 0).astype(jnp.float32), axis=0)


def gather(block, axis):
    count = lax.axis_size(axis)
    copies = jnp.broadcast_to(block[None], (count,) + block.shape)
    return lax.all_to_all(copies, axis, 0, 0).reshape((-1,) + block.shape[1:])


def project(embed, upstream):
    unit, inverse = normalize(embed)
    return inverse * (upstream - unit * jnp.sum(unit * upstream, axis=-1, keepdims=True))


def on_device(
    image_hidden,
    image_acts,
    image_proj,
    text_hidden,
    text_acts,
    text_proj,
    positives,
    log_scale,
    bias,
):
    rows = image_hidden.shape[0]
    total_rows = rows * lax.axis_size("img") * lax.axis_size("txt")
    image_sum = scatter_sum(
        jnp.dot(image_acts, image_proj, preferred_element_type=jnp.float32), "txt"
    )
    text_sum = scatter_sum(
        jnp.dot(text_acts, text_proj, preferred_element_type=jnp.float32), "img"
    )
    image_embed = (image_hidden.astype(jnp.float32) + image_sum).astype(jnp.bfloat16)
    text_embed = (text_hidden.astype(jnp.float32) + text_sum).astype(jnp.bfloat16)
    image_block = gather(image_embed, "txt")
    text_block = gather(text_embed, "img")
    image_unit = normalize(image_block)[0].astype(jnp.bfloat16)
    text_unit = normalize(text_block)[0].astype(jnp.bfloat16)
    scale = jnp.exp(log_scale[0])
    text_count = text_block.shape[0]
    scores = scale * contract_cols(image_unit, text_unit) + bias[0]
    columns = lax.axis_index("txt") * text_count + lax.broadcasted_iota(
        jnp.int32, (1, text_count), 1
    )
    target = (positives[:, None] == columns).astype(jnp.float32)
    partial_loss = jnp.sum(jax.nn.softplus((1.0 - 2.0 * target) * scores))
    slope = (jax.nn.sigmoid(scores) - target).astype(jnp.bfloat16)
    image_dir = scale * jnp.dot(slope, text_unit, preferred_element_type=jnp.float32)
    text_dir = scale * contract_rows(slope, image_unit)
    total = lax.psum(partial_loss, ("img", "txt"))
    loss = jnp.reshape(total / total_rows, (1,))
    image_grad = scatter_sum(project(image_block, image_dir), "txt").astype(jnp.bfloat16)
    text_grad = scatter_sum(project(text_block, text_dir), "img").astype(jnp.bfloat16)
    image_back = gather(image_grad, "txt")
    text_back = gather(text_grad, "img")
    image_act_grad = contract_cols(image_back, image_proj).astype(jnp.bfloat16)
    text_act_grad = contract_cols(text_back, text_proj).astype(jnp.bfloat16)
    image_proj_grad = scatter_sum(contract_rows(image_back, image_acts), "img").T
    text_proj_grad = scatter_sum(contract_rows(text_back, text_acts), "txt").T
    return (
        loss,
        image_grad,
        text_grad,
        image_act_grad,
        text_act_grad,
        image_proj_grad,
        text_proj_grad,
    )


def solution(mesh):
    return jax.shard_map(
        on_device,
        mesh=mesh,
        in_specs=(
            P(("img", "txt"), None),
            P("img", "txt"),
            P("txt", None),
            P(("txt", "img"), None),
            P("txt", "img"),
            P("img", None),
            P("img"),
            P(),
            P(),
        ),
        out_specs=(
            P(),
            P(("img", "txt"), None),
            P(("txt", "img"), None),
            P("img", "txt"),
            P("txt", "img"),
            P("txt", "img"),
            P("img", "txt"),
        ),
        check_vma=False,
    )
```

```python
import jax
import jax.numpy as jnp
from jax import lax
from jax.sharding import Mesh, PartitionSpec as P

AXES = ("z", "xl", "y", "xh", "c")
SIZES = (8, 2, 4, 2, 2)
IMG = ("z", "xl")
TXT = ("y", "xh", "c")
PLANE = ("xl", "y", "xh")
SWAP = [(0, 1), (1, 0)]
f32 = jnp.float32
bf16 = jnp.bfloat16


def normalize(embed):
    values = embed.astype(f32)
    inverse = lax.rsqrt(jnp.sum(values * values, axis=-1, keepdims=True) + 1e-06)
    return (values * inverse, inverse)


def project(embed, upstream):
    unit, inverse = normalize(embed)
    return inverse * (upstream - unit * jnp.sum(unit * upstream, axis=-1, keepdims=True))


def dot(left, right):
    return jnp.dot(left, right, preferred_element_type=f32)


def contract_rows(left, right):
    return lax.dot_general(left, right, (((0,), (0,)), ((), ())), preferred_element_type=f32)


def contract_cols(left, right):
    return lax.dot_general(left, right, (((1,), (1,)), ((), ())), preferred_element_type=f32)


def pick(blocks, index, axis=0):
    return lax.dynamic_index_in_dim(blocks, index, axis, keepdims=False)


def swap(block, axis):
    return lax.ppermute(block, axis, SWAP)


def pair(mine, other, index):
    return jnp.where(index == 0, jnp.stack([mine, other]), jnp.stack([other, mine]))


def shift(block, axis, step, count=4):
    return lax.ppermute(block, axis, [(i, (i + step) % count) for i in range(count)])


def plane_pairs(step, first):
    pairs = []
    for x in range(4):
        for y in range(4):
            for c in range(2):
                x2, y2 = ((x + step) % 4, y) if (c == 0) == first else (x, (y + step) % 4)
                pairs.append(
                    (((x % 2) * 4 + y) * 4 + (x // 2) * 2 + c, ((x2 % 2) * 4 + y2) * 4 + (x2 // 2) * 2 + c)
                )
    return pairs


def plane_shift(block, step, first):
    return lax.ppermute(block, ("xl", "y", "xh", "c"), plane_pairs(step % 4, first))


def plane_gather(block):
    row = jnp.stack([block] + [plane_shift(block, d, True) for d in (1, 2, 3)])
    slab = jnp.stack([row] + [plane_shift(row, d, False) for d in (1, 2, 3)])
    return jnp.stack([slab, swap(slab, "c")])


def plane_sum(parts):
    slab = (parts[0].astype(f32) + swap(parts[1], "c").astype(f32)).astype(bf16)
    row = slab[0].astype(f32)
    for d in (1, 2, 3):
        row = row + plane_shift(slab[d], -d, False).astype(f32)
    row = row.astype(bf16)
    total = row[0].astype(f32)
    for d in (1, 2, 3):
        total = total + plane_shift(row[d], -d, True).astype(f32)
    return total


def exchange(blocks, axis):
    return lax.all_to_all(blocks, axis, 0, 0)


def gather(block, axis):
    return exchange(jnp.broadcast_to(block[None], (lax.axis_size(axis),) + block.shape), axis)


def scatter_sum(blocks, axis):
    return jnp.sum(exchange(blocks, axis).astype(f32), axis=0)


def two_halves(value):
    high = lax.reduce_precision(value, 8, 7)
    return jnp.stack([high, value - high]).astype(bf16)


def with_loss(blocks, value):
    extra = jnp.broadcast_to(two_halves(value), blocks.shape[:-1] + (2,))
    return jnp.concatenate([blocks, extra], axis=-1)


def on_device(
    image_hidden,
    image_acts,
    image_proj,
    text_hidden,
    text_acts,
    text_proj,
    positives,
    log_scale,
    bias,
):
    z, xl, y, xh, c = [lax.axis_index(name) for name in AXES]
    rows, width = image_hidden.shape
    hidden = text_proj.shape[0]
    total_rows = rows * 256
    scale = jnp.exp(log_scale[0])

    acts_blocks = text_acts.reshape(8, 2, rows, hidden)
    acts_own = pick(acts_blocks, xl, 1).reshape(8 * rows, hidden)
    acts_near = swap(pick(acts_blocks, 1 - xl, 1).reshape(8 * rows, hidden), "xl")
    padded = jnp.pad(text_proj, ((0, 288 - hidden), (0, 0))).reshape(2, 144, width)
    proj_part = swap(pick(padded, c), "xl")
    proj_near = pair(proj_part, swap(proj_part, "c"), c).reshape(288, width)[:hidden]
    positives_near = swap(positives, "xl")

    parts = dot(image_acts, image_proj).astype(bf16).reshape(4, 2, 2, rows, width)
    parts = (pick(parts, c, 2).astype(f32) + swap(pick(parts, 1 - c, 2), "c").astype(f32)).astype(bf16)
    total = pick(parts, y).astype(f32)
    for d in (1, 2, 3):
        total = total + shift(pick(parts, (y + d) % 4), "y", d).astype(f32)
    total = total.astype(bf16)
    image_sum = pick(total, xh).astype(f32) + swap(pick(total, 1 - xh), "xh").astype(f32)
    image_embed = (image_hidden.astype(f32) + image_sum).astype(bf16)

    text_parts = dot(acts_own, text_proj) + dot(acts_near, proj_near)
    text_sum = scatter_sum(text_parts.astype(bf16).reshape(8, rows, width), "z")
    text_embed = (text_hidden.astype(f32) + text_sum).astype(bf16)

    image_block = plane_gather(image_embed).reshape(-1, width)
    text_block = gather(text_embed, "z").reshape(-1, width)
    image_unit = normalize(image_block)[0].astype(bf16)
    text_unit = normalize(text_block)[0].astype(bf16)

    labels = pair(positives, positives_near, xl).reshape(2, 4, 2, 2, rows)
    order = []
    x = xh * 2 + xl
    for k in range(2):
        core = c if k == 0 else 1 - c
        for e in range(4):
            for d in range(4):
                dx = jnp.where(core == 0, d, e)
                dy = jnp.where(core == 0, e, d)
                sx = (x - dx) % 4
                order.append((((sx % 2) * 4 + (y - dy) % 4) * 2 + sx // 2) * 2 + core)
    labels = jnp.take(labels.reshape(32, rows), jnp.stack(order), axis=0).reshape(-1)
    block_of = ((y * 2 + xh) * 2 + c) * 512 + xl * rows
    columns = block_of + jnp.arange(8, dtype=jnp.int32)[:, None] * (2 * rows)
    columns = (columns + jnp.arange(rows, dtype=jnp.int32)).reshape(1, -1)

    scores = scale * contract_cols(image_unit, text_unit) + bias[0]
    target = (labels[:, None] == columns).astype(f32)
    partial_loss = jnp.sum(jax.nn.softplus((1.0 - 2.0 * target) * scores))
    slope = (jax.nn.sigmoid(scores) - target).astype(bf16)
    text_dir = scale * contract_rows(slope, image_unit)
    image_dir = scale * dot(slope, text_unit)
    text_grad = scatter_sum(
        project(text_block, text_dir).astype(bf16).reshape(8, rows, width), "z"
    ).astype(bf16)
    image_grad = plane_sum(
        project(image_block, image_dir).astype(bf16).reshape(2, 4, 4, rows, width)
    ).astype(bf16)
    core_loss = partial_loss + swap(partial_loss, "c")

    near = pair(image_grad, swap(image_grad, "xh"), xh)
    ring = [near] + [shift(near, "y", d) for d in (3, 2, 1)]
    ring = lax.dynamic_slice_in_dim(jnp.stack(ring + ring), 4 - y, 4, 0)
    other = swap(ring, "c")
    image_back = jnp.where(c == 0, jnp.stack([ring, other], 2), jnp.stack([other, ring], 2))
    image_back = image_back.reshape(-1, width)
    image_act_grad = contract_cols(image_back, image_proj).astype(bf16)
    blocks = contract_rows(image_back, image_acts).astype(bf16).reshape(16, -1, hidden)
    found = exchange(with_loss(blocks, core_loss), IMG)
    image_proj_grad = jnp.sum(found[:, :, :hidden].astype(f32), axis=0).T
    core_loss = jnp.sum(found[:, 0, hidden:].astype(f32))

    text_back = gather(text_grad, "z").reshape(-1, width)
    act_grad_own = contract_cols(text_back, text_proj).astype(bf16)
    act_grad_near = swap(contract_cols(text_back, proj_near).astype(bf16), "xl")
    text_act_grad = jnp.where(
        xl == 0,
        jnp.stack([act_grad_own.reshape(8, rows, hidden), act_grad_near.reshape(8, rows, hidden)], 1),
        jnp.stack([act_grad_near.reshape(8, rows, hidden), act_grad_own.reshape(8, rows, hidden)], 1),
    ).reshape(-1, hidden)
    blocks_own = contract_rows(text_back, acts_own).astype(bf16).reshape(8, 2, -1, hidden)
    blocks_near = contract_rows(text_back, acts_near).astype(bf16).reshape(8, 2, -1, hidden)
    blocks = pair(blocks_own, blocks_near, xl)
    blocks = pick(blocks, c, 2).astype(f32) + swap(pick(blocks, 1 - c, 2), "c").astype(f32)
    blocks = blocks.astype(bf16).reshape(16, -1, hidden)
    found = exchange(with_loss(blocks, core_loss), PLANE)
    text_proj_grad = jnp.sum(found[:, :, :hidden].astype(f32), axis=0).T
    total_loss = 0.5 * jnp.sum(found[:, 0, hidden:].astype(f32))
    loss = jnp.reshape(total_loss / total_rows, (1,))
    return (
        loss,
        image_grad,
        text_grad,
        image_act_grad,
        text_act_grad,
        image_proj_grad,
        text_proj_grad,
    )


def solution(mesh):
    fine = Mesh(mesh.devices.reshape(SIZES), AXES)
    return jax.shard_map(
        on_device,
        mesh=fine,
        in_specs=(
            P(IMG + TXT, None),
            P(IMG, TXT),
            P(TXT, None),
            P(TXT + IMG, None),
            P(TXT, IMG),
            P(IMG, None),
            P(IMG),
            P(),
            P(),
        ),
        out_specs=(
            P(),
            P(IMG + TXT, None),
            P(TXT + IMG, None),
            P(IMG, TXT),
            P(TXT, IMG),
            P(TXT, IMG),
            P(IMG, TXT),
        ),
        check_vma=False,
    )
```

```python
import jax
import jax.numpy as jnp
from jax import lax
from jax.sharding import Mesh, PartitionSpec as P

AXES = ("z", "xl", "y", "xh", "c")
SIZES = (8, 2, 4, 2, 2)
IMG = ("z", "xl")
TXT = ("y", "xh", "c")
PLANE = ("xl", "y", "xh")
SWAP = [(0, 1), (1, 0)]
f32 = jnp.float32
bf16 = jnp.bfloat16


def normalize(embed):
    values = embed.astype(f32)
    inverse = lax.rsqrt(jnp.sum(values * values, axis=-1, keepdims=True) + 1e-06)
    return (values * inverse, inverse)


def project(embed, upstream):
    unit, inverse = normalize(embed)
    return inverse * (upstream - unit * jnp.sum(unit * upstream, axis=-1, keepdims=True))


def dot(left, right):
    return jnp.dot(left, right, preferred_element_type=f32)


def contract_rows(left, right):
    return lax.dot_general(left, right, (((0,), (0,)), ((), ())), preferred_element_type=f32)


def contract_cols(left, right):
    return lax.dot_general(left, right, (((1,), (1,)), ((), ())), preferred_element_type=f32)


def pick(blocks, index, axis=0):
    return lax.dynamic_index_in_dim(blocks, index, axis, keepdims=False)


def swap(block, axis):
    return lax.ppermute(block, axis, SWAP)


def pair(mine, other, index):
    return jnp.where(index == 0, jnp.stack([mine, other]), jnp.stack([other, mine]))


def shift(block, axis, step, count=4):
    return lax.ppermute(block, axis, [(i, (i + step) % count) for i in range(count)])


def plane_pairs(step, first):
    pairs = []
    for x in range(4):
        for y in range(4):
            for c in range(2):
                x2, y2 = ((x + step) % 4, y) if (c == 0) == first else (x, (y + step) % 4)
                pairs.append(
                    (((x % 2) * 4 + y) * 4 + (x // 2) * 2 + c, ((x2 % 2) * 4 + y2) * 4 + (x2 // 2) * 2 + c)
                )
    return pairs


def plane_shift(block, step, first):
    return lax.ppermute(block, ("xl", "y", "xh", "c"), plane_pairs(step % 4, first))


def plane_gather(block):
    row = jnp.stack([block] + [plane_shift(block, d, True) for d in (1, 2, 3)])
    slab = jnp.stack([row] + [plane_shift(row, d, False) for d in (1, 2, 3)])
    return jnp.stack([slab, swap(slab, "c")])


def plane_sum(parts, value):
    slab = parts[0].astype(f32) + swap(parts[1], "c").astype(f32)
    slab, value = lax.optimization_barrier((slab.astype(bf16), value + swap(value, "c")))
    row = slab[0].astype(f32)
    for d in (1, 2, 3):
        row = row + plane_shift(slab[d], -d, False).astype(f32)
    row, value = lax.optimization_barrier((row.astype(bf16), value + swap(value, "xh")))
    total = row[0].astype(f32)
    for d in (1, 2, 3):
        total = total + plane_shift(row[d], -d, True).astype(f32)
    return lax.optimization_barrier((total, value + flip_y(value, 1)))


def flip_y(value, bit):
    return lax.ppermute(value, "y", [(i, i ^ bit) for i in range(4)])


def exchange(blocks, axis):
    return lax.all_to_all(blocks, axis, 0, 0)


def gather(block, axis):
    return exchange(jnp.broadcast_to(block[None], (lax.axis_size(axis),) + block.shape), axis)


def scatter_sum(blocks, axis):
    return jnp.sum(exchange(blocks, axis).astype(f32), axis=0)


def two_halves(value):
    high = lax.reduce_precision(value, 8, 7)
    return jnp.stack([high, value - high]).astype(bf16)


def after(value, done):
    return lax.optimization_barrier((value, done))[0]


def on_device(
    image_hidden,
    image_acts,
    image_proj,
    text_hidden,
    text_acts,
    text_proj,
    positives,
    log_scale,
    bias,
):
    z, xl, y, xh, c = [lax.axis_index(name) for name in AXES]
    x = xh * 2 + xl
    rows, width = image_hidden.shape
    hidden = text_proj.shape[0]
    total_rows = rows * 256
    scale = jnp.exp(log_scale[0])

    text_parts = dot(text_acts, text_proj).astype(bf16).reshape(16, rows, width)
    text_sum = scatter_sum(text_parts, IMG)
    text_embed = (text_hidden.astype(f32) + text_sum).astype(bf16)

    image_acts = after(image_acts, text_parts)
    parts = dot(image_acts, image_proj).astype(bf16).reshape(4, 2, 2, rows, width)
    parts = (pick(parts, c, 2).astype(f32) + swap(pick(parts, 1 - c, 2), "c").astype(f32)).astype(bf16)
    total = pick(parts, y).astype(f32)
    for d in (1, 2, 3):
        total = total + shift(pick(parts, (y + d) % 4), "y", d).astype(f32)
    total = total.astype(bf16)
    image_sum = pick(total, xh).astype(f32) + swap(pick(total, 1 - xh), "xh").astype(f32)
    image_embed = (image_hidden.astype(f32) + image_sum).astype(bf16)

    image_block = plane_gather(after(image_embed, text_embed)).reshape(-1, width)
    text_block = gather(text_embed, "z").reshape(-1, width)
    image_unit = normalize(image_block)[0].astype(bf16)
    text_unit = normalize(text_block)[0].astype(bf16)

    positives_near = swap(positives, "xl")

    labels = pair(positives, positives_near, xl).reshape(2, 4, 2, 2, rows)
    order = []
    for k in range(2):
        core = c if k == 0 else 1 - c
        for e in range(4):
            for d in range(4):
                dx = jnp.where(core == 0, d, e)
                dy = jnp.where(core == 0, e, d)
                sx = (x - dx) % 4
                order.append((((sx % 2) * 4 + (y - dy) % 4) * 2 + sx // 2) * 2 + core)
    labels = jnp.take(labels.reshape(32, rows), jnp.stack(order), axis=0).reshape(-1)
    block_of = ((y * 2 + xh) * 2 + c) * 512 + xl * rows
    columns = block_of + jnp.arange(8, dtype=jnp.int32)[:, None] * (2 * rows)
    columns = (columns + jnp.arange(rows, dtype=jnp.int32)).reshape(1, -1)

    scores = scale * contract_cols(image_unit, text_unit) + bias[0]
    target = (labels[:, None] == columns).astype(f32)
    core_loss = jnp.sum(jax.nn.softplus((1.0 - 2.0 * target) * scores))
    slope = (jax.nn.sigmoid(scores) - target).astype(bf16)
    text_dir = scale * contract_rows(slope, image_unit)
    text_parts = project(text_block, text_dir).astype(bf16).reshape(8, rows, width)
    text_grad = scatter_sum(text_parts, "z").astype(bf16)

    image_dir = scale * dot(after(slope, text_parts), text_unit)
    image_parts = project(image_block, image_dir).astype(bf16)
    image_grad, core_loss = plane_sum(image_parts.reshape(2, 4, 4, rows, width), core_loss)
    image_grad = image_grad.astype(bf16)

    near = pair(image_grad, swap(image_grad, "xh"), xh)
    near, core_loss = lax.optimization_barrier((near, core_loss + flip_y(core_loss, 2)))
    ring = [near] + [shift(near, "y", d) for d in (3, 2, 1)]
    ring = lax.dynamic_slice_in_dim(jnp.stack(ring + ring), 4 - y, 4, 0)
    other = swap(ring, "c")
    image_back = jnp.where(c == 0, jnp.stack([ring, other], 2), jnp.stack([other, ring], 2))
    image_back = image_back.reshape(-1, width)
    wide_acts = jnp.pad(image_acts, ((0, 0), (0, 384 - hidden)))
    blocks = contract_rows(image_back, wide_acts).astype(bf16).reshape(16, -1, 384)
    extra = jnp.broadcast_to(two_halves(core_loss), (16, 1, 2))
    blocks = lax.dynamic_update_slice(blocks, extra, (0, 0, hidden))
    found = exchange(blocks, IMG)

    text_back = gather(after(text_grad, image_grad), IMG).reshape(-1, width)
    text_back = after(text_back, blocks)
    parts = contract_rows(text_back, text_acts).astype(bf16).reshape(4, 2, 2, -1, hidden)
    parts = (pick(parts, c, 2).astype(f32) + swap(pick(parts, 1 - c, 2), "c").astype(f32)).astype(bf16)
    total = pick(parts, y).astype(f32)
    for d in (1, 2, 3):
        total = total + shift(pick(parts, (y + d) % 4), "y", d).astype(f32)
    total = total.astype(bf16)
    text_proj_grad = pick(total, xh).astype(f32) + swap(pick(total, 1 - xh), "xh").astype(f32)
    text_proj_grad = text_proj_grad.T

    image_act_grad = contract_cols(after(image_back, parts), image_proj).astype(bf16)
    text_act_grad = contract_cols(after(text_back, parts), text_proj).astype(bf16)

    found = after(found, total).astype(f32)
    image_proj_grad = jnp.sum(found, axis=0)[:, :hidden].T
    total_loss = jnp.sum(found[:, 0, hidden : hidden + 2])
    loss = jnp.reshape(total_loss / total_rows, (1,))
    return (
        loss,
        image_grad,
        text_grad,
        image_act_grad,
        text_act_grad,
        image_proj_grad,
        text_proj_grad,
    )


def solution(mesh):
    fine = Mesh(mesh.devices.reshape(SIZES), AXES)
    return jax.shard_map(
        on_device,
        mesh=fine,
        in_specs=(
            P(IMG + TXT, None),
            P(IMG, TXT),
            P(TXT, None),
            P(TXT + IMG, None),
            P(TXT, IMG),
            P(IMG, None),
            P(IMG),
            P(),
            P(),
        ),
        out_specs=(
            P(),
            P(IMG + TXT, None),
            P(TXT + IMG, None),
            P(IMG, TXT),
            P(TXT, IMG),
            P(TXT, IMG),
            P(IMG, TXT),
        ),
        check_vma=False,
    )
```

```python
import functools

import jax
import jax.numpy as jnp
from jax import lax
from jax.experimental import pallas as pl
from jax.experimental.pallas import tpu as pltpu
from jax.sharding import Mesh, PartitionSpec as P

AXES = ("z", "xl", "y", "xh", "c")
SIZES = (8, 2, 4, 2, 2)
IMG = ("z", "xl")
TXT = ("y", "xh", "c")
PLANE = ("xl", "y", "xh")
SWAP = [(0, 1), (1, 0)]
f32 = jnp.float32
bf16 = jnp.bfloat16


def normalize(embed):
    values = embed.astype(f32)
    inverse = lax.rsqrt(jnp.sum(values * values, axis=-1, keepdims=True) + 1e-06)
    return (values * inverse, inverse)


def project(embed, upstream):
    unit, inverse = normalize(embed)
    return inverse * (upstream - unit * jnp.sum(unit * upstream, axis=-1, keepdims=True))


def dot(left, right):
    return jnp.dot(left, right, preferred_element_type=f32)


def contract_rows(left, right):
    return lax.dot_general(left, right, (((0,), (0,)), ((), ())), preferred_element_type=f32)


def contract_cols(left, right):
    return lax.dot_general(left, right, (((1,), (1,)), ((), ())), preferred_element_type=f32)


def pick(blocks, index, axis=0):
    return lax.dynamic_index_in_dim(blocks, index, axis, keepdims=False)


def swap(block, axis):
    return lax.ppermute(block, axis, SWAP)


def pair(mine, other, index):
    return jnp.where(index == 0, jnp.stack([mine, other]), jnp.stack([other, mine]))


def shift(block, axis, step, count=4):
    return lax.ppermute(block, axis, [(i, (i + step) % count) for i in range(count)])


def plane_pairs(step, first):
    pairs = []
    for x in range(4):
        for y in range(4):
            for c in range(2):
                x2, y2 = ((x + step) % 4, y) if (c == 0) == first else (x, (y + step) % 4)
                pairs.append(
                    (((x % 2) * 4 + y) * 4 + (x // 2) * 2 + c, ((x2 % 2) * 4 + y2) * 4 + (x2 // 2) * 2 + c)
                )
    return pairs


def plane_shift(block, step, first):
    return lax.ppermute(block, ("xl", "y", "xh", "c"), plane_pairs(step % 4, first))


def plane_gather(block, done):
    row = jnp.stack([block] + [plane_shift(block, d, True) for d in (1, 2, 3)])
    row = after(row, done)
    return jnp.stack([row] + [plane_shift(row, d, False) for d in (1, 2, 3)])


def plane_sum(slab):
    row = slab[0].astype(f32)
    for d in (1, 2, 3):
        row = row + plane_shift(slab[d], -d, False).astype(f32)
    row = row.astype(bf16)
    total = row[0].astype(f32)
    for d in (1, 2, 3):
        total = total + plane_shift(row[d], -d, True).astype(f32)
    return total


def exchange(blocks, axis):
    return lax.all_to_all(blocks, axis, 0, 0)


def gather(block, axis):
    return exchange(jnp.broadcast_to(block[None], (lax.axis_size(axis),) + block.shape), axis)


def scatter_sum(blocks, axis):
    return jnp.sum(exchange(blocks, axis).astype(f32), axis=0)


def two_halves(value):
    high = lax.reduce_precision(value, 8, 7)
    return jnp.stack([high, value - high]).astype(bf16)


CHUNK = 256
VMEM = pl.BlockSpec(memory_space=pltpu.VMEM)
SMEM = pl.BlockSpec(memory_space=pltpu.SMEM)


def score_rows(params, base, image, unit, labels, total, slope_out):
    scale, bias = params[0], params[1]
    index = lax.broadcasted_iota(jnp.int32, (unit.shape[0], 1), 0)
    columns = base[0] + index + (index & -32)
    loss = jnp.zeros((1, CHUNK), f32)
    for start in range(0, image.shape[0], CHUNK):
        part = pl.ds(start, CHUNK)
        image_unit = normalize(image[part, :])[0].astype(bf16)
        scores = scale * contract_cols(unit, image_unit) + bias
        hit = labels[:, part] == columns
        small = jnp.exp(-jnp.abs(scores))
        signed = jnp.where(hit, -scores, scores)
        terms = jnp.maximum(signed, 0.0) + jnp.log1p(small)
        loss = loss + jnp.sum(terms, axis=0, keepdims=True)
        sigmoid = jnp.where(scores >= 0.0, 1.0, small) / (1.0 + small)
        slope = (sigmoid - hit.astype(f32)).astype(bf16)
        slope_out[:, part] = slope
        total = total + dot(slope, image_unit)
    return total, loss


def score_kernel(params, base, image, text, labels, total_out, unit_out, slope_out, loss_out):
    unit = normalize(text[...])[0].astype(bf16)
    unit_out[...] = unit
    total = jnp.zeros(text.shape, f32)
    total, loss = score_rows(params, base, image, unit, labels, total, slope_out)
    total_out[...] = total
    loss_out[...] = loss


def rest_kernel(params, base, image, text, labels, total, unit, loss, parts_out, slope_out, loss_out):
    sums, more = score_rows(params, base, image, unit[...], labels, total[...], slope_out)
    parts_out[...] = project(text[...], params[0] * sums).astype(bf16)
    loss_out[...] = loss[...] + more


def image_kernel(params, slope, text_unit, image, image_parts):
    for start in range(0, image.shape[0], CHUNK):
        part = pl.ds(start, CHUNK)
        upstream = params[0] * contract_rows(slope[:, part], text_unit[...])
        image_parts[part, :] = project(image[part, :], upstream).astype(bf16)


def like(array, dtype):
    return jax.ShapeDtypeStruct(array.shape, dtype)


def score_call(params, base, image, text, labels):
    return pl.pallas_call(
        score_kernel,
        out_shape=(
            like(text, f32),
            like(text, bf16),
            jax.ShapeDtypeStruct((text.shape[0], image.shape[0]), bf16),
            jax.ShapeDtypeStruct((1, CHUNK), f32),
        ),
        in_specs=[SMEM, SMEM, VMEM, VMEM, VMEM],
        out_specs=(VMEM, VMEM, VMEM, VMEM),
        compiler_params=pltpu.CompilerParams(vmem_limit_bytes=24 * 2**20),
        name="score",
    )(params, base, image, text, labels)


def rest_call(params, base, image, text, labels, total, unit, loss):
    return pl.pallas_call(
        rest_kernel,
        out_shape=(
            like(text, bf16),
            jax.ShapeDtypeStruct((text.shape[0], image.shape[0]), bf16),
            like(loss, f32),
        ),
        in_specs=[SMEM, SMEM, VMEM, VMEM, VMEM, VMEM, VMEM, VMEM],
        out_specs=(VMEM, VMEM, VMEM),
        compiler_params=pltpu.CompilerParams(vmem_limit_bytes=24 * 2**20),
        name="score_rest",
    )(params, base, image, text, labels, total, unit, loss)


def weight_kernel(hidden, place, own, other, acts, back, blocks):
    y, c = place[0], place[1]
    rows, width = back.shape[-2:]
    loss = jnp.zeros((1, 128), f32)
    for d in range(4):
        at = lax.rem(y - d + 4, 4)
        for k in range(2):
            back[at, k, c] = own[d, k, :rows]
            back[at, k, 1 - c] = other[d, k, :rows]
            for part in (own, other):
                loss = loss + part[d, k, rows:].astype(f32)[:1, :128]
    total = jnp.sum(loss, axis=1, keepdims=True)
    high = total.astype(bf16).astype(f32)
    product = contract_rows(back[...].reshape(-1, width), acts[...])
    count, height = blocks.shape[:2]
    row = lax.broadcasted_iota(jnp.int32, (height, blocks.shape[2]), 0)
    lane = lax.broadcasted_iota(jnp.int32, (height, blocks.shape[2]), 1)
    first = jnp.where(lane == hidden, high, jnp.where(lane == hidden + 1, total - high, 0.0))
    first = jnp.where(row == 0, first, 0.0)
    for k in range(count):
        blocks[k] = (product[k * height : (k + 1) * height] + first).astype(bf16)


def weight_call(place, own, other, acts, rows, hidden):
    width = own.shape[-1]
    return pl.pallas_call(
        functools.partial(weight_kernel, hidden),
        out_shape=(
            jax.ShapeDtypeStruct((4, 2, 2, rows, width), bf16),
            jax.ShapeDtypeStruct((16, width // 16, acts.shape[1]), bf16),
        ),
        in_specs=[SMEM, VMEM, VMEM, VMEM],
        out_specs=(VMEM, VMEM),
        compiler_params=pltpu.CompilerParams(vmem_limit_bytes=24 * 2**20),
        name="image_weight",
    )(place, own, other, acts)


def text_weight_kernel(place, back, acts, mine, theirs):
    product = contract_rows(back[...], acts[...])
    height = mine.shape[2]
    for k in range(8):
        left = product[2 * k * height : (2 * k + 1) * height]
        right = product[(2 * k + 1) * height : (2 * k + 2) * height]
        mine[k // 2, k % 2] = jnp.where(place[1] == 0, left, right).astype(bf16)
        theirs[k // 2, k % 2] = jnp.where(place[1] == 0, right, left).astype(bf16)


def text_weight_call(place, back, acts):
    shape = jax.ShapeDtypeStruct((4, 2, back.shape[1] // 16, acts.shape[1]), bf16)
    return pl.pallas_call(
        text_weight_kernel,
        out_shape=(shape, shape),
        in_specs=[SMEM, VMEM, VMEM],
        out_specs=(VMEM, VMEM),
        compiler_params=pltpu.CompilerParams(vmem_limit_bytes=24 * 2**20),
        name="text_weight",
    )(place, back, acts)


def image_call(params, slope, text_unit, image):
    return pl.pallas_call(
        image_kernel,
        out_shape=jax.ShapeDtypeStruct(image.shape, bf16),
        in_specs=[SMEM, VMEM, VMEM, VMEM],
        out_specs=VMEM,
        compiler_params=pltpu.CompilerParams(vmem_limit_bytes=16 * 2**20),
        name="image_direction",
    )(params, slope, text_unit, image)


def after(value, done):
    return lax.optimization_barrier((value, done))[0]


def on_device(
    image_hidden,
    image_acts,
    image_proj,
    text_hidden,
    text_acts,
    text_proj,
    positives,
    log_scale,
    bias,
):
    z, xl, y, xh, c = [lax.axis_index(name) for name in AXES]
    x = xh * 2 + xl
    rows, width = image_hidden.shape
    hidden = text_proj.shape[0]
    total_rows = rows * 256
    scale = jnp.exp(log_scale[0])

    text_parts = dot(text_acts, text_proj).astype(bf16).reshape(16, rows, width)
    text_sum = scatter_sum(text_parts, IMG)
    text_embed = (text_hidden.astype(f32) + text_sum).astype(bf16)

    image_acts = after(image_acts, text_parts)
    parts = dot(image_acts, image_proj).astype(bf16).reshape(4, 2, 2, rows, width)
    parts = (pick(parts, c, 2).astype(f32) + swap(pick(parts, 1 - c, 2), "c").astype(f32)).astype(bf16)
    total = pick(parts, y).astype(f32)
    for d in (1, 2, 3):
        total = total + shift(pick(parts, (y + d) % 4), "y", d).astype(f32)
    total = total.astype(bf16)
    image_sum = pick(total, xh).astype(f32) + swap(pick(total, 1 - xh), "xh").astype(f32)
    image_embed = (image_hidden.astype(f32) + image_sum).astype(bf16)

    own_block = plane_gather(image_embed, text_embed).reshape(-1, width)
    text_block = gather(text_embed, "z").reshape(-1, width)
    near_block = swap(after(own_block, text_block), "c")

    positives_near = swap(positives, "xl")

    labels = pair(positives, positives_near, xl).reshape(2, 4, 2, 2, rows)
    order = []
    for k in range(2):
        core = c if k == 0 else 1 - c
        for e in range(4):
            for d in range(4):
                dx = jnp.where(core == 0, d, e)
                dy = jnp.where(core == 0, e, d)
                sx = (x - dx) % 4
                order.append((((sx % 2) * 4 + (y - dy) % 4) * 2 + sx // 2) * 2 + core)
    labels = jnp.take(labels.reshape(32, rows), jnp.stack(order), axis=0).reshape(1, -1)
    base = jnp.reshape(((y * 2 + xh) * 2 + c) * 512 + xl * rows, (1,)).astype(jnp.int32)
    params = jnp.stack([scale, bias[0]])
    half = 16 * rows
    text_total, text_unit, own_slope, losses = score_call(
        params, base, own_block, text_block, labels[:, :half]
    )
    text_parts, near_slope, losses = rest_call(
        params, base, near_block, text_block, labels[:, half:], text_total, text_unit, losses
    )
    text_grad = scatter_sum(text_parts.reshape(8, rows, width), "z").astype(bf16)

    theirs = swap(image_call(params, near_slope, text_unit, near_block), "c")
    mine = image_call(params, own_slope, text_unit, after(own_block, text_parts))
    halves = jnp.pad(two_halves(jnp.sum(losses))[None], ((0, 7), (0, width - 2)))
    slab = (mine.astype(f32) + theirs.astype(f32)).astype(bf16)
    image_grad = plane_sum(slab.reshape(4, 4, rows, width))
    image_grad = image_grad.astype(bf16)

    near = jnp.concatenate([image_grad, halves])
    near = pair(near, swap(near, "xh"), xh)
    ring = jnp.stack([near] + [shift(near, "y", d) for d in (1, 2, 3)])
    place = jnp.stack([y, c]).astype(jnp.int32)
    wide = ((0, 0), (0, 384 - hidden))
    image_back, blocks = weight_call(place, ring, swap(ring, "c"), jnp.pad(image_acts, wide), rows, hidden)
    image_back = image_back.reshape(-1, width)
    found = exchange(blocks, IMG)

    text_back = gather(after(text_grad, image_grad), IMG).reshape(-1, width)
    text_back = after(text_back, blocks)
    mine, theirs = text_weight_call(place, text_back, jnp.pad(text_acts, wide))
    parts = (mine.astype(f32) + swap(theirs, "c").astype(f32)).astype(bf16)
    total = pick(parts, y).astype(f32)
    for d in (1, 2, 3):
        total = total + shift(pick(parts, (y + d) % 4), "y", d).astype(f32)
    total = total.astype(bf16)
    text_proj_grad = pick(total, xh).astype(f32) + swap(pick(total, 1 - xh), "xh").astype(f32)
    text_proj_grad = text_proj_grad[:, :hidden].T

    image_act_grad = contract_cols(after(image_back, parts), image_proj).astype(bf16)
    text_act_grad = contract_cols(after(text_back, parts), text_proj).astype(bf16)

    found = after(found, total).astype(f32)
    image_proj_grad = jnp.sum(found, axis=0)[:, :hidden].T
    total_loss = jnp.sum(found[:, 0, hidden : hidden + 2])
    loss = jnp.reshape(total_loss / total_rows, (1,))
    return (
        loss,
        image_grad,
        text_grad,
        image_act_grad,
        text_act_grad,
        image_proj_grad,
        text_proj_grad,
    )


def solution(mesh):
    fine = Mesh(mesh.devices.reshape(SIZES), AXES)
    return jax.shard_map(
        on_device,
        mesh=fine,
        in_specs=(
            P(IMG + TXT, None),
            P(IMG, TXT),
            P(TXT, None),
            P(TXT + IMG, None),
            P(TXT, IMG),
            P(IMG, None),
            P(IMG),
            P(),
            P(),
        ),
        out_specs=(
            P(),
            P(IMG + TXT, None),
            P(TXT + IMG, None),
            P(IMG, TXT),
            P(TXT, IMG),
            P(TXT, IMG),
            P(IMG, TXT),
        ),
        check_vma=False,
    )
```

```python
import functools

import jax
import jax.numpy as jnp
from jax import lax
from jax.experimental import pallas as pl
from jax.experimental.pallas import tpu as pltpu
from jax.sharding import Mesh, PartitionSpec as P

AXES = ("z", "xl", "y", "xh", "c")
SIZES = (8, 2, 4, 2, 2)
IMG = ("z", "xl")
TXT = ("y", "xh", "c")
PLANE = ("xl", "y", "xh")
SWAP = [(0, 1), (1, 0)]
f32 = jnp.float32
bf16 = jnp.bfloat16


def normalize(embed):
    values = embed.astype(f32)
    inverse = lax.rsqrt(jnp.sum(values * values, axis=-1, keepdims=True) + 1e-06)
    return (values * inverse, inverse)


def project(embed, upstream):
    unit, inverse = normalize(embed)
    return inverse * (upstream - unit * jnp.sum(unit * upstream, axis=-1, keepdims=True))


def dot(left, right):
    return jnp.dot(left, right, preferred_element_type=f32)


def contract_rows(left, right):
    return lax.dot_general(left, right, (((0,), (0,)), ((), ())), preferred_element_type=f32)


def contract_cols(left, right):
    return lax.dot_general(left, right, (((1,), (1,)), ((), ())), preferred_element_type=f32)


def pick(blocks, index, axis=0):
    return lax.dynamic_index_in_dim(blocks, index, axis, keepdims=False)


def swap(block, axis):
    return lax.ppermute(block, axis, SWAP)


def pair(mine, other, index):
    return jnp.where(index == 0, jnp.stack([mine, other]), jnp.stack([other, mine]))


def shift(block, axis, step, count=4):
    return lax.ppermute(block, axis, [(i, (i + step) % count) for i in range(count)])


def plane_pairs(step, first):
    pairs = []
    for x in range(4):
        for y in range(4):
            for c in range(2):
                x2, y2 = ((x + step) % 4, y) if (c == 0) == first else (x, (y + step) % 4)
                pairs.append(
                    (((x % 2) * 4 + y) * 4 + (x // 2) * 2 + c, ((x2 % 2) * 4 + y2) * 4 + (x2 // 2) * 2 + c)
                )
    return pairs


def plane_shift(block, step, first):
    return lax.ppermute(block, ("xl", "y", "xh", "c"), plane_pairs(step % 4, first))


def gather_first(block):
    return jnp.stack([block] + [plane_shift(block, d, True) for d in (1, 2, 3)])


def gather_second(row):
    return jnp.stack([row] + [plane_shift(row, d, False) for d in (1, 2, 3)])


def sum_second(slab):
    total = slab[0].astype(f32)
    for d in (1, 2, 3):
        total = total + plane_shift(slab[d], -d, False).astype(f32)
    return total.astype(bf16)


def sum_first(row):
    total = row[0].astype(f32)
    for d in (1, 2, 3):
        total = total + plane_shift(row[d], -d, True).astype(f32)
    return total.astype(bf16)


def exchange(blocks, axis):
    return lax.all_to_all(blocks, axis, 0, 0)


def gather(block, axis):
    return exchange(jnp.broadcast_to(block[None], (lax.axis_size(axis),) + block.shape), axis)


def scatter_sum(blocks, axis):
    return jnp.sum(exchange(blocks, axis).astype(f32), axis=0)


CHUNK = 256
VMEM = pl.BlockSpec(memory_space=pltpu.VMEM)
SMEM = pl.BlockSpec(memory_space=pltpu.SMEM)


def score_rows(params, base, image, unit, labels, total, image_parts):
    scale, bias = params[0], params[1]
    index = lax.broadcasted_iota(jnp.int32, (unit.shape[0], 1), 0)
    columns = base[0] + index + (index & -32)
    loss = jnp.zeros((1, CHUNK), f32)
    for start in range(0, image.shape[0], CHUNK):
        part = pl.ds(start, CHUNK)
        wide_unit, inverse = normalize(image[part, :])
        image_unit = wide_unit.astype(bf16)
        scores = scale * contract_cols(unit, image_unit) + bias
        hit = labels[:, part] == columns
        small = jnp.exp(-jnp.abs(scores))
        signed = jnp.where(hit, -scores, scores)
        terms = jnp.maximum(signed, 0.0) + jnp.log1p(small)
        loss = loss + jnp.sum(terms, axis=0, keepdims=True)
        sigmoid = jnp.where(scores >= 0.0, 1.0, small) / (1.0 + small)
        slope = (sigmoid - hit.astype(f32)).astype(bf16)
        total = total + dot(slope, image_unit)
        upstream = scale * contract_rows(slope, unit)
        along = jnp.sum(wide_unit * upstream, axis=-1, keepdims=True)
        image_parts[part, :] = (inverse * (upstream - wide_unit * along)).astype(bf16)
    return total, loss


def score_kernel(params, base, image, text, labels, total_out, unit_out, image_parts, loss_out):
    unit = normalize(text[...])[0].astype(bf16)
    unit_out[...] = unit
    total = jnp.zeros(text.shape, f32)
    total, loss = score_rows(params, base, image, unit, labels, total, image_parts)
    total_out[...] = total
    loss_out[...] = loss


def rest_kernel(params, base, image, text, labels, total, unit, loss, text_parts, image_parts, halves):
    sums, more = score_rows(params, base, image, unit[...], labels, total[...], image_parts)
    text_parts[...] = project(text[...], params[0] * sums).astype(bf16)
    sums = jnp.sum(loss[...] + more, axis=1, keepdims=True)
    high = sums.astype(bf16).astype(f32)
    lane = lax.broadcasted_iota(jnp.int32, halves.shape, 1)
    values = jnp.where(lane == 0, high, jnp.where(lane == 1, sums - high, 0.0))
    halves[...] = values.astype(bf16)


def like(array, dtype):
    return jax.ShapeDtypeStruct(array.shape, dtype)


def score_call(params, base, image, text, labels):
    return pl.pallas_call(
        score_kernel,
        out_shape=(
            like(text, f32),
            like(text, bf16),
            like(image, bf16),
            jax.ShapeDtypeStruct((1, CHUNK), f32),
        ),
        in_specs=[SMEM, SMEM, VMEM, VMEM, VMEM],
        out_specs=(VMEM, VMEM, VMEM, VMEM),
        compiler_params=pltpu.CompilerParams(vmem_limit_bytes=24 * 2**20),
        name="score",
    )(params, base, image, text, labels)


def rest_call(params, base, image, text, labels, total, unit, loss):
    return pl.pallas_call(
        rest_kernel,
        out_shape=(
            like(text, bf16),
            like(image, bf16),
            jax.ShapeDtypeStruct((8, text.shape[1]), bf16),
        ),
        in_specs=[SMEM, SMEM, VMEM, VMEM, VMEM, VMEM, VMEM, VMEM],
        out_specs=(VMEM, VMEM, VMEM),
        compiler_params=pltpu.CompilerParams(vmem_limit_bytes=24 * 2**20),
        name="score_rest",
    )(params, base, image, text, labels, total, unit, loss)


def packed(grad, acts, hidden, high, low):
    main = lax.dot_general(
        grad, acts[:256, :], (((0,), (1,)), ((), ())), preferred_element_type=f32
    )
    tail = dot(acts[256:, :], grad)
    row = lax.broadcasted_iota(jnp.int32, tail.shape, 0)
    tail = jnp.where(row == hidden - 256, high, jnp.where(row == hidden - 255, low, tail))
    width = grad.shape[1]
    height = width // 16
    for k in range(16):
        left, right = [
            pltpu.roll(half, (width - k * height) % width, 1)[:, :128] for half in (tail[:8], tail[8:])
        ]
        below = jnp.concatenate([left, right], axis=1)
        yield jnp.concatenate([main[k * height : (k + 1) * height], below], axis=0)


def finish_kernel(hidden, blocks, grad, value):
    total = jnp.zeros(blocks.shape[1:], f32)
    for k in range(blocks.shape[0]):
        total = total + blocks[k].astype(f32)
    height = grad.shape[0]
    grad[:, :256] = total[:height]
    tail = jnp.concatenate([total[height:, :128], total[height:, 128:]])
    grad[:, 256:] = tail.T[:height, : hidden - 256]
    value[...] = tail[hidden - 256 : hidden - 255, :1] + tail[hidden - 255 : hidden - 254, :1]


def finish_call(blocks, hidden):
    grad, value = pl.pallas_call(
        functools.partial(finish_kernel, hidden),
        out_shape=(
            jax.ShapeDtypeStruct((blocks.shape[1] - 8, hidden), f32),
            jax.ShapeDtypeStruct((1, 1), f32),
        ),
        in_specs=[VMEM],
        out_specs=(VMEM, VMEM),
        compiler_params=pltpu.CompilerParams(vmem_limit_bytes=16 * 2**20),
        name="finish",
    )(blocks)
    return grad.T, value


def weight_kernel(hidden, place, own, other, acts, back, blocks):
    y, c = place[0], place[1]
    rows, width = back.shape[-2:]
    loss = jnp.zeros((1, 128), f32)
    for d in range(4):
        at = lax.rem(y - d + 4, 4)
        for k in range(2):
            back[at, k, c] = own[d, k, :rows]
            back[at, k, 1 - c] = other[d, k, :rows]
            for part in (own, other):
                loss = loss + part[d, k, rows:].astype(f32)[:1, :128]
    total = jnp.sum(loss, axis=1, keepdims=True)
    high = total.astype(bf16).astype(f32)
    for k, block in enumerate(packed(back[...].reshape(-1, width), acts, hidden, high, total - high)):
        blocks[k] = block.astype(bf16)


def weight_call(place, own, other, acts, rows, hidden):
    width = own.shape[-1]
    return pl.pallas_call(
        functools.partial(weight_kernel, hidden),
        out_shape=(
            jax.ShapeDtypeStruct((4, 2, 2, rows, width), bf16),
            jax.ShapeDtypeStruct((16, width // 16 + 8, 256), bf16),
        ),
        in_specs=[SMEM, VMEM, VMEM, VMEM],
        out_specs=(VMEM, VMEM),
        compiler_params=pltpu.CompilerParams(vmem_limit_bytes=24 * 2**20),
        name="image_weight",
    )(place, own, other, acts)


def text_weight_kernel(hidden, place, back, acts, mine, theirs):
    blocks = list(packed(back[...], acts, hidden, 0.0, 0.0))
    for k in range(8):
        left, right = blocks[2 * k], blocks[2 * k + 1]
        mine[k // 2, k % 2] = jnp.where(place[1] == 0, left, right).astype(bf16)
        theirs[k // 2, k % 2] = jnp.where(place[1] == 0, right, left).astype(bf16)


def text_weight_call(place, back, acts, hidden):
    shape = jax.ShapeDtypeStruct((4, 2, back.shape[1] // 16 + 8, 256), bf16)
    return pl.pallas_call(
        functools.partial(text_weight_kernel, hidden),
        out_shape=(shape, shape),
        in_specs=[SMEM, VMEM, VMEM],
        out_specs=(VMEM, VMEM),
        compiler_params=pltpu.CompilerParams(vmem_limit_bytes=24 * 2**20),
        name="text_weight",
    )(place, back, acts)


def after(value, done):
    return lax.optimization_barrier((value, done))[0]


def on_device(
    image_hidden,
    image_acts,
    image_proj,
    text_hidden,
    text_acts,
    text_proj,
    positives,
    log_scale,
    bias,
):
    z, xl, y, xh, c = [lax.axis_index(name) for name in AXES]
    x = xh * 2 + xl
    rows, width = image_hidden.shape
    hidden = text_proj.shape[0]
    total_rows = rows * 256
    scale = jnp.exp(log_scale[0])

    text_parts = dot(text_acts, text_proj).astype(bf16).reshape(16, rows, width)
    text_sum = scatter_sum(text_parts, IMG)
    text_embed = (text_hidden.astype(f32) + text_sum).astype(bf16)

    image_acts = after(image_acts, text_parts)
    parts = dot(image_acts, image_proj).astype(bf16).reshape(4, 2, 2, rows, width)
    parts = (pick(parts, c, 2).astype(f32) + swap(pick(parts, 1 - c, 2), "c").astype(f32)).astype(bf16)
    total = pick(parts, y).astype(f32)
    for d in (1, 2, 3):
        total = total + shift(pick(parts, (y + d) % 4), "y", d).astype(f32)
    total = total.astype(bf16)
    image_sum = pick(total, xh).astype(f32) + swap(pick(total, 1 - xh), "xh").astype(f32)
    image_embed = (image_hidden.astype(f32) + image_sum).astype(bf16)

    positives_near = swap(positives, "xl")
    labels = pair(positives, positives_near, xl).reshape(2, 4, 2, 2, rows)
    n = jnp.arange(32, dtype=jnp.int32)
    core = jnp.where(n < 16, c, 1 - c)
    e, d = n // 4 % 4, n % 4
    from_x = (x - jnp.where(core == 0, d, e)) & 3
    from_y = (y - jnp.where(core == 0, e, d)) & 3
    order = (((from_x % 2) * 4 + from_y) * 2 + from_x // 2) * 2 + core
    labels = jnp.take(labels.reshape(32, rows), order, axis=0).reshape(1, -1)
    base = jnp.reshape(((y * 2 + xh) * 2 + c) * 512 + xl * rows, (1,)).astype(jnp.int32)
    image_row = gather_first(image_embed)
    text_block = gather(after(text_embed, (image_row, labels)), "z").reshape(-1, width)
    own_block = gather_second(after(image_row, text_embed)).reshape(-1, width)
    near_block = swap(after(own_block, text_block), "c")

    params = jnp.stack([scale, bias[0]])
    half = 16 * rows
    text_total, text_unit, mine, losses = score_call(
        params, base, own_block, text_block, labels[:, :half]
    )
    text_parts, theirs, halves = rest_call(
        params, base, near_block, text_block, labels[:, half:], text_total, text_unit, losses
    )
    text_grad = scatter_sum(text_parts.reshape(8, rows, width), "z").astype(bf16)
    theirs = swap(theirs, "c")
    slab = (mine.astype(f32) + theirs.astype(f32)).astype(bf16)
    image_row = sum_second(slab.reshape(4, 4, rows, width))
    image_grad = sum_first(image_row)

    near = jnp.concatenate([image_grad, halves])
    near = pair(near, swap(near, "xh"), xh)
    ring = jnp.stack([near] + [shift(near, "y", d) for d in (1, 2, 3)])
    place = jnp.stack([y, c]).astype(jnp.int32)
    wide = ((0, 272 - hidden), (0, 0))
    image_back, blocks = weight_call(place, ring, swap(ring, "c"), jnp.pad(image_acts.T, wide), rows, hidden)
    image_back = image_back.reshape(-1, width)
    found = exchange(blocks, IMG)

    text_back = gather(after(text_grad, image_row), IMG).reshape(-1, width)
    text_back = after(text_back, blocks)
    mine, theirs = text_weight_call(place, text_back, jnp.pad(text_acts.T, wide), hidden)
    parts = (mine.astype(f32) + swap(theirs, "c").astype(f32)).astype(bf16)
    total = pick(parts, y).astype(f32)
    for d in (1, 2, 3):
        total = total + shift(pick(parts, (y + d) % 4), "y", d).astype(f32)
    total = total.astype(bf16)
    last = jnp.stack([pick(total, xh), swap(pick(total, 1 - xh), "xh")])

    image_act_grad = contract_cols(after(image_back, parts), image_proj).astype(bf16)
    text_act_grad = contract_cols(after(text_back, parts), text_proj).astype(bf16)

    text_proj_grad = finish_call(last, hidden)[0]
    image_proj_grad, total_loss = finish_call(after(found, last), hidden)
    loss = jnp.reshape(total_loss / total_rows, (1,))
    return (
        loss,
        image_grad,
        text_grad,
        image_act_grad,
        text_act_grad,
        image_proj_grad,
        text_proj_grad,
    )


def solution(mesh):
    fine = Mesh(mesh.devices.reshape(SIZES), AXES)
    return jax.shard_map(
        on_device,
        mesh=fine,
        in_specs=(
            P(IMG + TXT, None),
            P(IMG, TXT),
            P(TXT, None),
            P(TXT + IMG, None),
            P(TXT, IMG),
            P(IMG, None),
            P(IMG),
            P(),
            P(),
        ),
        out_specs=(
            P(),
            P(IMG + TXT, None),
            P(TXT + IMG, None),
            P(IMG, TXT),
            P(TXT, IMG),
            P(TXT, IMG),
            P(IMG, TXT),
        ),
        check_vma=False,
    )
```

```python
import functools

import jax
import jax.numpy as jnp
from jax import lax
from jax.experimental import pallas as pl
from jax.experimental.pallas import tpu as pltpu
from jax.sharding import Mesh, PartitionSpec as P

AXES = ("z", "xl", "y", "xh", "c")
SIZES = (8, 2, 4, 2, 2)
IMG = ("z", "xl")
TXT = ("y", "xh", "c")
PLANE = ("xl", "y", "xh")
SWAP = [(0, 1), (1, 0)]
f32 = jnp.float32
bf16 = jnp.bfloat16


def normalize(embed):
    values = embed.astype(f32)
    inverse = lax.rsqrt(jnp.sum(values * values, axis=-1, keepdims=True) + 1e-06)
    return (values * inverse, inverse)


def project(embed, upstream):
    unit, inverse = normalize(embed)
    return inverse * (upstream - unit * jnp.sum(unit * upstream, axis=-1, keepdims=True))


def dot(left, right):
    return jnp.dot(left, right, preferred_element_type=f32)


def contract_rows(left, right):
    return lax.dot_general(left, right, (((0,), (0,)), ((), ())), preferred_element_type=f32)


def contract_cols(left, right):
    return lax.dot_general(left, right, (((1,), (1,)), ((), ())), preferred_element_type=f32)


def pick(blocks, index, axis=0):
    return lax.dynamic_index_in_dim(blocks, index, axis, keepdims=False)


def swap(block, axis):
    return lax.ppermute(block, axis, SWAP)


def pair(mine, other, index):
    return jnp.where(index == 0, jnp.stack([mine, other]), jnp.stack([other, mine]))


def shift(block, axis, step, count=4):
    return lax.ppermute(block, axis, [(i, (i + step) % count) for i in range(count)])


def gather_y(block):
    return jnp.stack([block] + [shift(block, "y", d) for d in (1, 2, 3)])


def sum_y(blocks):
    total = blocks[0].astype(f32)
    for d in (1, 2, 3):
        total = total + shift(blocks[d], "y", 4 - d).astype(f32)
    return total.astype(bf16)


def turn_x(block, a, b):
    return lax.ppermute(block, ("xl", "xh"), [(i, i ^ (2 * a + b)) for i in range(4)])


def exchange(blocks, axis):
    return lax.all_to_all(blocks, axis, 0, 0)


def spread_kernel(parts, base, row, copies):
    total = base[...].astype(f32)
    for k in range(parts.shape[0]):
        total = total + parts[k].astype(f32)
    total = total.astype(bf16)
    row[...] = total
    for k in range(copies.shape[0]):
        copies[k] = total


def spread_call(parts, base, count):
    return pl.pallas_call(
        spread_kernel,
        out_shape=(
            jax.ShapeDtypeStruct(base.shape, bf16),
            jax.ShapeDtypeStruct((count,) + base.shape, bf16),
        ),
        in_specs=[VMEM, VMEM],
        out_specs=(VMEM, VMEM),
        compiler_params=pltpu.CompilerParams(vmem_limit_bytes=8 * 2**20),
        name="spread",
    )(parts, base)


CHUNK = 256
VMEM = pl.BlockSpec(memory_space=pltpu.VMEM)
SMEM = pl.BlockSpec(memory_space=pltpu.SMEM)


def score_rows(params, base, image, unit, labels, total, image_parts):
    scale, bias = params[0], params[1]
    index = lax.broadcasted_iota(jnp.int32, (unit.shape[0], 1), 0)
    columns = base[0] + index + (index & -32)
    loss = jnp.zeros((1, CHUNK), f32)
    for start in range(0, image.shape[0], CHUNK):
        part = pl.ds(start, CHUNK)
        wide_unit, inverse = normalize(image[part, :])
        image_unit = wide_unit.astype(bf16)
        scores = scale * contract_cols(unit, image_unit) + bias
        hit = labels[:, part] == columns
        small = jnp.exp(-jnp.abs(scores))
        signed = jnp.where(hit, -scores, scores)
        terms = jnp.maximum(signed, 0.0) + jnp.log1p(small)
        loss = loss + jnp.sum(terms, axis=0, keepdims=True)
        sigmoid = jnp.where(scores >= 0.0, 1.0, small) / (1.0 + small)
        slope = (sigmoid - hit.astype(f32)).astype(bf16)
        total = total + dot(slope, image_unit)
        upstream = scale * contract_rows(slope, unit)
        along = jnp.sum(wide_unit * upstream, axis=-1, keepdims=True)
        image_parts[part, :] = (inverse * (upstream - wide_unit * along)).astype(bf16)
    return total, loss


def score_kernel(params, base, image, text, labels, total_out, unit_out, image_parts, loss_out):
    unit = normalize(text[...])[0].astype(bf16)
    unit_out[...] = unit
    total = jnp.zeros(text.shape, f32)
    total, loss = score_rows(params, base, image, unit, labels, total, image_parts)
    total_out[...] = total
    loss_out[...] = loss


def rest_kernel(params, base, image, text, labels, total, unit, loss, text_parts, image_parts, halves):
    sums, more = score_rows(params, base, image, unit[...], labels, total[...], image_parts)
    text_parts[...] = project(text[...], params[0] * sums).astype(bf16)
    sums = jnp.sum(loss[...] + more, axis=1, keepdims=True)
    high = sums.astype(bf16).astype(f32)
    lane = lax.broadcasted_iota(jnp.int32, halves.shape, 1)
    row = lax.broadcasted_iota(jnp.int32, halves.shape, 0)
    values = jnp.where(lane == 0, high, jnp.where(lane == 1, sums - high, 0.0))
    halves[...] = jnp.where(row == base[1], values, 0.0).astype(bf16)


def like(array, dtype):
    return jax.ShapeDtypeStruct(array.shape, dtype)


def score_call(params, base, image, text, labels):
    return pl.pallas_call(
        score_kernel,
        out_shape=(
            like(text, f32),
            like(text, bf16),
            like(image, bf16),
            jax.ShapeDtypeStruct((1, CHUNK), f32),
        ),
        in_specs=[SMEM, SMEM, VMEM, VMEM, VMEM],
        out_specs=(VMEM, VMEM, VMEM, VMEM),
        compiler_params=pltpu.CompilerParams(vmem_limit_bytes=14 * 2**20),
        name="score",
    )(params, base, image, text, labels)


def rest_call(params, base, image, text, labels, total, unit, loss):
    return pl.pallas_call(
        rest_kernel,
        out_shape=(
            like(text, bf16),
            like(image, bf16),
            jax.ShapeDtypeStruct((8, text.shape[1]), bf16),
        ),
        in_specs=[SMEM, SMEM, VMEM, VMEM, VMEM, VMEM, VMEM, VMEM],
        out_specs=(VMEM, VMEM, VMEM),
        compiler_params=pltpu.CompilerParams(vmem_limit_bytes=14 * 2**20),
        name="score_rest",
    )(params, base, image, text, labels, total, unit, loss)


def packed(grad, acts, hidden, high, low):
    main = lax.dot_general(
        grad, acts[:256, :], (((0,), (1,)), ((), ())), preferred_element_type=f32
    )
    tail = dot(acts[256:, :], grad)
    row = lax.broadcasted_iota(jnp.int32, tail.shape, 0)
    tail = jnp.where(row == hidden - 256, high, jnp.where(row == hidden - 255, low, tail))
    width = grad.shape[1]
    height = width // 16
    for k in range(16):
        left, right = [
            pltpu.roll(half, (width - k * height) % width, 1)[:, :128] for half in (tail[:8], tail[8:])
        ]
        below = jnp.concatenate([left, right], axis=1)
        yield jnp.concatenate([main[k * height : (k + 1) * height], below], axis=0)


def finish_kernel(hidden, blocks, grad, value):
    total = jnp.zeros(blocks.shape[1:], f32)
    for k in range(blocks.shape[0]):
        total = total + blocks[k].astype(f32)
    height = grad.shape[0]
    grad[:, :256] = total[:height]
    tail = jnp.concatenate([total[height:, :128], total[height:, 128:]])
    grad[:, 256:] = tail.T[:height, : hidden - 256]
    value[...] = tail[hidden - 256 : hidden - 255, :1] + tail[hidden - 255 : hidden - 254, :1]


def finish_call(blocks, hidden):
    grad, value = pl.pallas_call(
        functools.partial(finish_kernel, hidden),
        out_shape=(
            jax.ShapeDtypeStruct((blocks.shape[1] - 8, hidden), f32),
            jax.ShapeDtypeStruct((1, 1), f32),
        ),
        in_specs=[VMEM],
        out_specs=(VMEM, VMEM),
        compiler_params=pltpu.CompilerParams(vmem_limit_bytes=6 * 2**20),
        name="finish",
    )(blocks)
    return grad.T, value


def weight_kernel(hidden, place, own, other, acts, proj, act_grad, blocks, back):
    y, c = place[0], place[1]
    rows, width = back.shape[-2:]
    loss = jnp.zeros((8, 128), f32)
    for d in range(4):
        at = lax.rem(y - d + 4, 4)
        for k in range(2):
            back[at, k, c] = own[d, k, :rows]
            back[at, k, 1 - c] = other[d, k, :rows]
            for part in (own, other):
                loss = loss + part[d, k, rows:].astype(f32)[:, :128]
    total = jnp.sum(jnp.sum(loss, axis=1, keepdims=True), axis=0, keepdims=True)
    high = total.astype(bf16).astype(f32)
    grad = back[...].reshape(-1, width)
    for k, block in enumerate(packed(grad, acts, hidden, high, total - high)):
        blocks[k] = block.astype(bf16)
    act_grad[...] = contract_cols(proj[...], grad).astype(bf16)


def weight_call(place, own, other, acts, proj, rows):
    hidden, width = proj.shape
    return pl.pallas_call(
        functools.partial(weight_kernel, hidden),
        out_shape=(
            jax.ShapeDtypeStruct((hidden, acts.shape[1]), bf16),
            jax.ShapeDtypeStruct((16, width // 16 + 8, 256), bf16),
        ),
        in_specs=[SMEM, VMEM, VMEM, VMEM, VMEM],
        out_specs=(VMEM, VMEM),
        scratch_shapes=[pltpu.VMEM((4, 2, 2, rows, width), bf16)],
        compiler_params=pltpu.CompilerParams(vmem_limit_bytes=16 * 2**20),
        name="image_weight",
    )(place, own, other, acts, proj)


def text_weight_kernel(hidden, place, back, acts, proj, act_grad, mine, theirs):
    blocks = list(packed(back[...], acts, hidden, 0.0, 0.0))
    for k in range(8):
        left, right = blocks[2 * k], blocks[2 * k + 1]
        mine[k // 2, k % 2] = jnp.where(place[1] == 0, left, right).astype(bf16)
        theirs[k // 2, k % 2] = jnp.where(place[1] == 0, right, left).astype(bf16)
    act_grad[...] = contract_cols(proj[...], back[...]).astype(bf16)


def text_weight_call(place, back, acts, proj):
    hidden, width = proj.shape
    shape = jax.ShapeDtypeStruct((4, 2, width // 16 + 8, 256), bf16)
    return pl.pallas_call(
        functools.partial(text_weight_kernel, hidden),
        out_shape=(jax.ShapeDtypeStruct((hidden, acts.shape[1]), bf16), shape, shape),
        in_specs=[SMEM, VMEM, VMEM, VMEM],
        out_specs=(VMEM, VMEM, VMEM),
        compiler_params=pltpu.CompilerParams(vmem_limit_bytes=16 * 2**20),
        name="text_weight",
    )(place, back, acts, proj)


def after(value, done):
    return lax.optimization_barrier((value, done))[0]


def on_device(
    image_hidden,
    image_acts,
    image_proj,
    text_hidden,
    text_acts,
    text_proj,
    positives,
    log_scale,
    bias,
):
    z, xl, y, xh, c = [lax.axis_index(name) for name in AXES]
    rows, width = image_hidden.shape
    hidden = text_proj.shape[0]
    total_rows = rows * 256
    scale = jnp.exp(log_scale[0])

    text_parts = dot(text_acts, text_proj).astype(bf16).reshape(16, rows, width)
    text_embed, copies = spread_call(exchange(text_parts, IMG), text_hidden, 8)

    image_acts = after(image_acts, text_parts)
    parts = dot(image_acts, image_proj).astype(bf16).reshape(4, 2, 2, rows, width)
    parts = (pick(parts, c, 2).astype(f32) + swap(pick(parts, 1 - c, 2), "c").astype(f32)).astype(bf16)
    total = pick(parts, y).astype(f32)
    for d in (1, 2, 3):
        total = total + shift(pick(parts, (y + d) % 4), "y", d).astype(f32)
    here = (jnp.arange(2, dtype=jnp.int32) == xh)[:, None, None]
    total = (total + jnp.where(here, image_hidden.astype(f32)[None], 0.0)).astype(bf16)
    image_row = jnp.stack(
        [
            total.astype(f32) + turn_x(total, 0, 1).astype(f32),
            turn_x(total, 1, 0).astype(f32) + turn_x(total, 1, 1).astype(f32),
        ]
    ).astype(bf16)

    positives_near = swap(positives, "xl")
    labels = pair(positives, positives_near, xl).reshape(2, 4, 2, 2, rows)
    n = jnp.arange(32, dtype=jnp.int32)
    core = jnp.where(n < 16, c, 1 - c)
    from_y = (y - n // 4 % 4) & 3
    order = (((xl ^ (n // 2 % 2)) * 4 + from_y) * 2 + n % 2) * 2 + core
    labels = jnp.take(labels.reshape(32, rows), order, axis=0).reshape(1, -1)
    base = jnp.stack([((y * 2 + xh) * 2 + c) * 512 + xl * rows, xl * 2 + xh]).astype(jnp.int32)
    params = jnp.stack([scale, bias[0]])
    text_block = exchange(after(copies, (image_row, labels, params, base)), "z").reshape(-1, width)
    own_block = gather_y(after(image_row, text_embed)).reshape(-1, width)
    near_block = swap(after(own_block, text_block), "c")

    half = 16 * rows
    text_total, text_unit, mine, losses = score_call(
        params, base, own_block, text_block, labels[:, :half]
    )
    text_parts, theirs, halves = rest_call(
        params, base, near_block, text_block, labels[:, half:], text_total, text_unit, losses
    )
    text_grad, copies = spread_call(
        exchange(text_parts.reshape(8, rows, width), "z"), jnp.zeros((rows, width), bf16), 16
    )
    theirs = swap(theirs, "c")
    slab = (mine.astype(f32) + theirs.astype(f32)).astype(bf16)
    image_row = sum_y(slab.reshape(4, 4, rows, width)).reshape(2, 2, rows, width)

    image_row = after(image_row, text_grad)
    halves = jnp.broadcast_to(halves, (2, 2) + halves.shape)
    image_row = jnp.concatenate([image_row, halves], axis=2)
    near = image_row[0].astype(f32) + turn_x(image_row[0], 0, 1).astype(f32)
    near = near + turn_x(image_row[1], 1, 0).astype(f32) + turn_x(image_row[1], 1, 1).astype(f32)
    near = near.astype(bf16)
    image_grad = pick(near, xh)[:rows]
    ring = gather_y(near)
    place = jnp.stack([y, c]).astype(jnp.int32)
    wide = ((0, 272 - hidden), (0, 0))
    image_act_grad, blocks = weight_call(
        place, ring, swap(ring, "c"), jnp.pad(image_acts.T, wide), image_proj, rows
    )
    found = exchange(blocks, IMG)

    text_back = exchange(after(copies, image_row), IMG).reshape(-1, width)
    text_back = after(text_back, blocks)
    text_act_grad, mine, theirs = text_weight_call(
        place, text_back, jnp.pad(text_acts.T, wide), text_proj
    )
    parts = (mine.astype(f32) + swap(theirs, "c").astype(f32)).astype(bf16)
    total = pick(parts, y).astype(f32)
    for d in (1, 2, 3):
        total = total + shift(pick(parts, (y + d) % 4), "y", d).astype(f32)
    total = total.astype(bf16)
    last = jnp.stack([pick(total, xh), swap(pick(total, 1 - xh), "xh")])

    text_proj_grad = finish_call(last, hidden)[0]
    image_proj_grad, total_loss = finish_call(after(found, last), hidden)
    loss = jnp.reshape(0.25 * total_loss / total_rows, (1,))
    return (
        loss,
        image_grad,
        text_grad,
        image_act_grad.T,
        text_act_grad.T,
        image_proj_grad,
        text_proj_grad,
    )


def solution(mesh):
    fine = Mesh(mesh.devices.reshape(SIZES), AXES)
    return jax.shard_map(
        on_device,
        mesh=fine,
        in_specs=(
            P(IMG + TXT, None),
            P(IMG, TXT),
            P(TXT, None),
            P(TXT + IMG, None),
            P(TXT, IMG),
            P(IMG, None),
            P(IMG),
            P(),
            P(),
        ),
        out_specs=(
            P(),
            P(IMG + TXT, None),
            P(TXT + IMG, None),
            P(IMG, TXT),
            P(TXT, IMG),
            P(TXT, IMG),
            P(IMG, TXT),
        ),
        check_vma=False,
    )
```

```python
import functools

import jax
import jax.numpy as jnp
from jax import lax
from jax.experimental import pallas as pl
from jax.experimental.pallas import tpu as pltpu
from jax.sharding import Mesh, PartitionSpec as P

AXES = ("z", "xl", "y", "xh", "c")
SIZES = (8, 2, 4, 2, 2)
IMG = ("z", "xl")
TXT = ("y", "xh", "c")
PLANE = ("xl", "y", "xh")
SWAP = [(0, 1), (1, 0)]
f32 = jnp.float32
bf16 = jnp.bfloat16


def normalize(embed):
    values = embed.astype(f32)
    inverse = lax.rsqrt(jnp.sum(values * values, axis=-1, keepdims=True) + 1e-06)
    return (values * inverse, inverse)


def project(embed, upstream):
    unit, inverse = normalize(embed)
    return inverse * (upstream - unit * jnp.sum(unit * upstream, axis=-1, keepdims=True))


def dot(left, right):
    return jnp.dot(left, right, preferred_element_type=f32)


def contract_rows(left, right):
    return lax.dot_general(left, right, (((0,), (0,)), ((), ())), preferred_element_type=f32)


def contract_cols(left, right):
    return lax.dot_general(left, right, (((1,), (1,)), ((), ())), preferred_element_type=f32)


def pick(blocks, index, axis=0):
    return lax.dynamic_index_in_dim(blocks, index, axis, keepdims=False)


def swap(block, axis):
    return lax.ppermute(block, axis, SWAP)


def pair(mine, other, index):
    return jnp.where(index == 0, jnp.stack([mine, other]), jnp.stack([other, mine]))


def shift(block, axis, step, count=4):
    return lax.ppermute(block, axis, [(i, (i + step) % count) for i in range(count)])


def gather_y(block):
    return jnp.stack([block] + [shift(block, "y", d) for d in (1, 2, 3)])


def sum_y(blocks):
    total = blocks[0].astype(f32)
    for d in (1, 2, 3):
        total = total + shift(blocks[d], "y", 4 - d).astype(f32)
    return total.astype(bf16)


def turn_x(block, a, b):
    return lax.ppermute(block, ("xl", "xh"), [(i, i ^ (2 * a + b)) for i in range(4)])


def exchange(blocks, axis):
    return lax.all_to_all(blocks, axis, 0, 0)


def spread_kernel(parts, base, row, copies):
    total = base[...].astype(f32)
    for k in range(parts.shape[0]):
        total = total + parts[k].astype(f32)
    total = total.astype(bf16)
    row[...] = total
    for k in range(copies.shape[0]):
        copies[k] = total


def spread_call(parts, base, count):
    return pl.pallas_call(
        spread_kernel,
        out_shape=(
            jax.ShapeDtypeStruct(base.shape, bf16),
            jax.ShapeDtypeStruct((count,) + base.shape, bf16),
        ),
        in_specs=[VMEM, VMEM],
        out_specs=(VMEM, VMEM),
        compiler_params=pltpu.CompilerParams(vmem_limit_bytes=8 * 2**20),
        name="spread",
    )(parts, base)


CHUNK = 512
VMEM = pl.BlockSpec(memory_space=pltpu.VMEM)
SMEM = pl.BlockSpec(memory_space=pltpu.SMEM)


def score_rows(params, base, image, unit, labels, total, image_parts):
    scale, bias = params[0], params[1]
    index = lax.broadcasted_iota(jnp.int32, (unit.shape[0], 1), 0)
    columns = base[0] + index + (index & -32)
    loss = jnp.zeros((1, CHUNK), f32)
    for start in range(0, image.shape[0], CHUNK):
        part = pl.ds(start, CHUNK)
        wide_unit, inverse = normalize(image[part, :])
        image_unit = wide_unit.astype(bf16)
        scores = scale * contract_cols(unit, image_unit) + bias
        hit = labels[:, part] == columns
        small = jnp.exp(-jnp.abs(scores))
        signed = jnp.where(hit, -scores, scores)
        loss = loss + jnp.sum(jnp.maximum(signed, 0.0), axis=0, keepdims=True)
        product = small
        for _ in range(3):
            height = product.shape[0] // 2
            upper, lower = product[:height], product[height:]
            product = upper + lower + upper * lower
        loss = loss + jnp.sum(jnp.log1p(product), axis=0, keepdims=True)
        sigmoid = jnp.where(scores >= 0.0, 1.0, small) / (1.0 + small)
        slope = (sigmoid - hit.astype(f32)).astype(bf16)
        total = total + dot(slope, image_unit)
        upstream = contract_rows(slope, unit)
        along = jnp.sum(wide_unit * upstream, axis=-1, keepdims=True)
        image_parts[part, :] = (scale * inverse * (upstream - wide_unit * along)).astype(bf16)
    return total, loss


def score_kernel(params, base, image, text, labels, total_out, unit_out, image_parts, loss_out):
    unit = normalize(text[...])[0].astype(bf16)
    unit_out[...] = unit
    total = jnp.zeros(text.shape, f32)
    total, loss = score_rows(params, base, image, unit, labels, total, image_parts)
    total_out[...] = total
    loss_out[...] = loss


def rest_kernel(params, base, image, text, labels, total, unit, loss, text_parts, image_parts, halves):
    sums, more = score_rows(params, base, image, unit[...], labels, total[...], image_parts)
    text_parts[...] = project(text[...], params[0] * sums).astype(bf16)
    sums = jnp.sum(loss[...] + more, axis=1, keepdims=True)
    high = sums.astype(bf16).astype(f32)
    lane = lax.broadcasted_iota(jnp.int32, halves.shape, 1)
    row = lax.broadcasted_iota(jnp.int32, halves.shape, 0)
    values = jnp.where(lane == 0, high, jnp.where(lane == 1, sums - high, 0.0))
    halves[...] = jnp.where(row == base[1], values, 0.0).astype(bf16)


def like(array, dtype):
    return jax.ShapeDtypeStruct(array.shape, dtype)


def score_call(params, base, image, text, labels):
    return pl.pallas_call(
        score_kernel,
        out_shape=(
            like(text, f32),
            like(text, bf16),
            like(image, bf16),
            jax.ShapeDtypeStruct((1, CHUNK), f32),
        ),
        in_specs=[SMEM, SMEM, VMEM, VMEM, VMEM],
        out_specs=(VMEM, VMEM, VMEM, VMEM),
        compiler_params=pltpu.CompilerParams(vmem_limit_bytes=14 * 2**20),
        name="score",
    )(params, base, image, text, labels)


def rest_call(params, base, image, text, labels, total, unit, loss):
    return pl.pallas_call(
        rest_kernel,
        out_shape=(
            like(text, bf16),
            like(image, bf16),
            jax.ShapeDtypeStruct((8, text.shape[1]), bf16),
        ),
        in_specs=[SMEM, SMEM, VMEM, VMEM, VMEM, VMEM, VMEM, VMEM],
        out_specs=(VMEM, VMEM, VMEM),
        compiler_params=pltpu.CompilerParams(vmem_limit_bytes=14 * 2**20),
        name="score_rest",
    )(params, base, image, text, labels, total, unit, loss)


def packed(grad, acts, hidden, high, low):
    main = lax.dot_general(
        grad, acts[:256, :], (((0,), (1,)), ((), ())), preferred_element_type=f32
    )
    tail = dot(acts[256:, :], grad)
    row = lax.broadcasted_iota(jnp.int32, tail.shape, 0)
    tail = jnp.where(row == hidden - 256, high, jnp.where(row == hidden - 255, low, tail))
    width = grad.shape[1]
    height = width // 16
    for k in range(16):
        left, right = [
            pltpu.roll(half, (width - k * height) % width, 1)[:, :128] for half in (tail[:8], tail[8:])
        ]
        below = jnp.concatenate([left, right], axis=1)
        yield jnp.concatenate([main[k * height : (k + 1) * height], below], axis=0)


def finish_kernel(hidden, blocks, grad, value):
    total = jnp.zeros(blocks.shape[1:], f32)
    for k in range(blocks.shape[0]):
        total = total + blocks[k].astype(f32)
    height = grad.shape[0]
    grad[:, :256] = total[:height]
    tail = jnp.concatenate([total[height:, :128], total[height:, 128:]])
    grad[:, 256:] = tail.T[:height, : hidden - 256]
    value[...] = tail[hidden - 256 : hidden - 255, :1] + tail[hidden - 255 : hidden - 254, :1]


def finish_call(blocks, hidden):
    grad, value = pl.pallas_call(
        functools.partial(finish_kernel, hidden),
        out_shape=(
            jax.ShapeDtypeStruct((blocks.shape[1] - 8, hidden), f32),
            jax.ShapeDtypeStruct((1, 1), f32),
        ),
        in_specs=[VMEM],
        out_specs=(VMEM, VMEM),
        compiler_params=pltpu.CompilerParams(vmem_limit_bytes=6 * 2**20),
        name="finish",
    )(blocks)
    return grad.T, value


def weight_kernel(hidden, place, own, other, acts, proj, act_grad, blocks, back):
    y, c = place[0], place[1]
    rows, width = back.shape[-2:]
    loss = jnp.zeros((8, 128), f32)
    for d in range(4):
        at = lax.rem(y - d + 4, 4)
        for k in range(2):
            back[at, k, c] = own[d, k, :rows]
            back[at, k, 1 - c] = other[d, k, :rows]
            for part in (own, other):
                loss = loss + part[d, k, rows:].astype(f32)[:, :128]
    total = jnp.sum(jnp.sum(loss, axis=1, keepdims=True), axis=0, keepdims=True)
    high = total.astype(bf16).astype(f32)
    grad = back[...].reshape(-1, width)
    for k, block in enumerate(packed(grad, acts, hidden, high, total - high)):
        blocks[k] = block.astype(bf16)
    act_grad[...] = contract_cols(proj[...], grad).astype(bf16)


def weight_call(place, own, other, acts, proj, rows):
    hidden, width = proj.shape
    return pl.pallas_call(
        functools.partial(weight_kernel, hidden),
        out_shape=(
            jax.ShapeDtypeStruct((hidden, acts.shape[1]), bf16),
            jax.ShapeDtypeStruct((16, width // 16 + 8, 256), bf16),
        ),
        in_specs=[SMEM, VMEM, VMEM, VMEM, VMEM],
        out_specs=(VMEM, VMEM),
        scratch_shapes=[pltpu.VMEM((4, 2, 2, rows, width), bf16)],
        compiler_params=pltpu.CompilerParams(vmem_limit_bytes=16 * 2**20),
        name="image_weight",
    )(place, own, other, acts, proj)


def text_weight_kernel(hidden, place, back, acts, proj, act_grad, mine, theirs):
    blocks = list(packed(back[...], acts, hidden, 0.0, 0.0))
    for k in range(8):
        left, right = blocks[2 * k], blocks[2 * k + 1]
        mine[k // 2, k % 2] = jnp.where(place[1] == 0, left, right).astype(bf16)
        theirs[k // 2, k % 2] = jnp.where(place[1] == 0, right, left).astype(bf16)
    act_grad[...] = contract_cols(proj[...], back[...]).astype(bf16)


def text_weight_call(place, back, acts, proj):
    hidden, width = proj.shape
    shape = jax.ShapeDtypeStruct((4, 2, width // 16 + 8, 256), bf16)
    return pl.pallas_call(
        functools.partial(text_weight_kernel, hidden),
        out_shape=(jax.ShapeDtypeStruct((hidden, acts.shape[1]), bf16), shape, shape),
        in_specs=[SMEM, VMEM, VMEM, VMEM],
        out_specs=(VMEM, VMEM, VMEM),
        compiler_params=pltpu.CompilerParams(vmem_limit_bytes=16 * 2**20),
        name="text_weight",
    )(place, back, acts, proj)


def after(value, done):
    return lax.optimization_barrier((value, done))[0]


def on_device(
    image_hidden,
    image_acts,
    image_proj,
    text_hidden,
    text_acts,
    text_proj,
    positives,
    log_scale,
    bias,
):
    z, xl, y, xh, c = [lax.axis_index(name) for name in AXES]
    rows, width = image_hidden.shape
    hidden = text_proj.shape[0]
    total_rows = rows * 256
    scale = jnp.exp(log_scale[0])

    text_parts = dot(text_acts, text_proj).astype(bf16).reshape(16, rows, width)
    text_embed, copies = spread_call(exchange(text_parts, IMG), text_hidden, 8)

    image_acts = after(image_acts, text_parts)
    parts = dot(image_acts, image_proj).astype(bf16).reshape(4, 2, 2, rows, width)
    parts = (pick(parts, c, 2).astype(f32) + swap(pick(parts, 1 - c, 2), "c").astype(f32)).astype(bf16)
    total = pick(parts, y).astype(f32)
    for d in (1, 2, 3):
        total = total + shift(pick(parts, (y + d) % 4), "y", d).astype(f32)
    here = (jnp.arange(2, dtype=jnp.int32) == xh)[:, None, None]
    total = (total + jnp.where(here, image_hidden.astype(f32)[None], 0.0)).astype(bf16)
    image_row = jnp.stack(
        [
            total.astype(f32) + turn_x(total, 0, 1).astype(f32),
            turn_x(total, 1, 0).astype(f32) + turn_x(total, 1, 1).astype(f32),
        ]
    ).astype(bf16)

    positives_near = swap(positives, "xl")
    labels = pair(positives, positives_near, xl).reshape(2, 4, 2, 2, rows)
    n = jnp.arange(32, dtype=jnp.int32)
    core = jnp.where(n < 16, c, 1 - c)
    from_y = (y - n // 4 % 4) & 3
    order = (((xl ^ (n // 2 % 2)) * 4 + from_y) * 2 + n % 2) * 2 + core
    labels = jnp.take(labels.reshape(32, rows), order, axis=0).reshape(1, -1)
    base = jnp.stack([((y * 2 + xh) * 2 + c) * 512 + xl * rows, xl * 2 + xh]).astype(jnp.int32)
    params = jnp.stack([scale, bias[0]])
    text_block = exchange(after(copies, (image_row, labels, params, base)), "z").reshape(-1, width)
    own_block = gather_y(after(image_row, text_embed)).reshape(-1, width)
    near_block = swap(after(own_block, text_block), "c")

    half = 16 * rows
    text_total, text_unit, mine, losses = score_call(
        params, base, own_block, text_block, labels[:, :half]
    )
    text_parts, theirs, halves = rest_call(
        params, base, near_block, text_block, labels[:, half:], text_total, text_unit, losses
    )
    text_grad, copies = spread_call(
        exchange(text_parts.reshape(8, rows, width), "z"), jnp.zeros((rows, width), bf16), 16
    )
    theirs = swap(theirs, "c")
    slab = (mine.astype(f32) + theirs.astype(f32)).astype(bf16)
    image_row = sum_y(slab.reshape(4, 4, rows, width)).reshape(2, 2, rows, width)

    image_row = after(image_row, text_grad)
    halves = jnp.broadcast_to(halves, (2, 2) + halves.shape)
    image_row = jnp.concatenate([image_row, halves], axis=2)
    near = image_row[0].astype(f32) + turn_x(image_row[0], 0, 1).astype(f32)
    near = near + turn_x(image_row[1], 1, 0).astype(f32) + turn_x(image_row[1], 1, 1).astype(f32)
    near = near.astype(bf16)
    image_grad = pick(near, xh)[:rows]
    ring = gather_y(near)
    place = jnp.stack([y, c]).astype(jnp.int32)
    wide = ((0, 272 - hidden), (0, 0))
    image_act_grad, blocks = weight_call(
        place, ring, swap(ring, "c"), jnp.pad(image_acts.T, wide), image_proj, rows
    )
    found = exchange(blocks, IMG)

    text_back = exchange(after(copies, image_row), IMG).reshape(-1, width)
    text_back = after(text_back, blocks)
    text_act_grad, mine, theirs = text_weight_call(
        place, text_back, jnp.pad(text_acts.T, wide), text_proj
    )
    parts = (mine.astype(f32) + swap(theirs, "c").astype(f32)).astype(bf16)
    total = pick(parts, y).astype(f32)
    for d in (1, 2, 3):
        total = total + shift(pick(parts, (y + d) % 4), "y", d).astype(f32)
    total = total.astype(bf16)
    last = jnp.stack([pick(total, xh), swap(pick(total, 1 - xh), "xh")])

    text_proj_grad = finish_call(last, hidden)[0]
    image_proj_grad, total_loss = finish_call(after(found, last), hidden)
    loss = jnp.reshape(0.25 * total_loss / total_rows, (1,))
    return (
        loss,
        image_grad,
        text_grad,
        image_act_grad.T,
        text_act_grad.T,
        image_proj_grad,
        text_proj_grad,
    )


def solution(mesh):
    fine = Mesh(mesh.devices.reshape(SIZES), AXES)
    return jax.shard_map(
        on_device,
        mesh=fine,
        in_specs=(
            P(IMG + TXT, None),
            P(IMG, TXT),
            P(TXT, None),
            P(TXT + IMG, None),
            P(TXT, IMG),
            P(IMG, None),
            P(IMG),
            P(),
            P(),
        ),
        out_specs=(
            P(),
            P(IMG + TXT, None),
            P(TXT + IMG, None),
            P(IMG, TXT),
            P(TXT, IMG),
            P(TXT, IMG),
            P(IMG, TXT),
        ),
        check_vma=False,
    )
```

```python
import functools

import jax
import jax.numpy as jnp
from jax import lax
from jax.experimental import pallas as pl
from jax.experimental.pallas import tpu as pltpu
from jax.sharding import Mesh, PartitionSpec as P

AXES = ("z", "xl", "y", "xh", "c")
SIZES = (8, 2, 4, 2, 2)
IMG = ("z", "xl")
TXT = ("y", "xh", "c")
PLANE = ("xl", "y", "xh")
SWAP = [(0, 1), (1, 0)]
f32 = jnp.float32
bf16 = jnp.bfloat16


def normalize(embed):
    values = embed.astype(f32)
    inverse = lax.rsqrt(jnp.sum(values * values, axis=-1, keepdims=True) + 1e-06)
    return (values * inverse, inverse)


def project(embed, upstream):
    unit, inverse = normalize(embed)
    return inverse * (upstream - unit * jnp.sum(unit * upstream, axis=-1, keepdims=True))


def dot(left, right):
    return jnp.dot(left, right, preferred_element_type=f32)


def contract_rows(left, right):
    return lax.dot_general(left, right, (((0,), (0,)), ((), ())), preferred_element_type=f32)


def contract_cols(left, right):
    return lax.dot_general(left, right, (((1,), (1,)), ((), ())), preferred_element_type=f32)


def pick(blocks, index, axis=0):
    return lax.dynamic_index_in_dim(blocks, index, axis, keepdims=False)


def swap(block, axis):
    return lax.ppermute(block, axis, SWAP)


def pair(mine, other, index):
    return jnp.where(index == 0, jnp.stack([mine, other]), jnp.stack([other, mine]))


def shift(block, axis, step, count=4):
    return lax.ppermute(block, axis, [(i, (i + step) % count) for i in range(count)])


def gather_y(block):
    return jnp.stack([block] + [shift(block, "y", d) for d in (1, 2, 3)])


def sum_y(blocks):
    total = blocks[0].astype(f32)
    for d in (1, 2, 3):
        total = total + shift(blocks[d], "y", 4 - d).astype(f32)
    return total.astype(bf16)


def turn_x(block, a, b):
    return lax.ppermute(block, ("xl", "xh"), [(i, i ^ (2 * a + b)) for i in range(4)])


def exchange(blocks, axis):
    return lax.all_to_all(blocks, axis, 0, 0)


def spread_kernel(parts, base, row, copies):
    total = base[...].astype(f32)
    for k in range(parts.shape[0]):
        total = total + parts[k].astype(f32)
    total = total.astype(bf16)
    row[...] = total
    for k in range(copies.shape[0]):
        copies[k] = total


def spread_call(parts, base, count):
    return pl.pallas_call(
        spread_kernel,
        out_shape=(
            jax.ShapeDtypeStruct(base.shape, bf16),
            jax.ShapeDtypeStruct((count,) + base.shape, bf16),
        ),
        in_specs=[VMEM, VMEM],
        out_specs=(VMEM, VMEM),
        compiler_params=pltpu.CompilerParams(vmem_limit_bytes=8 * 2**20),
        name="spread",
    )(parts, base)


CHUNK = 512
VMEM = pl.BlockSpec(memory_space=pltpu.VMEM)
SMEM = pl.BlockSpec(memory_space=pltpu.SMEM)


def score_rows(params, base, image, unit, labels, total, image_parts):
    scale, bias = params[0], params[1]
    index = lax.broadcasted_iota(jnp.int32, (unit.shape[0], 1), 0)
    columns = base[0] + index + (index & -32)
    loss = jnp.zeros((1, CHUNK), f32)
    for start in range(0, image.shape[0], CHUNK):
        part = pl.ds(start, CHUNK)
        wide_unit, inverse = normalize(image[part, :])
        image_unit = wide_unit.astype(bf16)
        scores = scale * contract_cols(unit, image_unit) + bias
        hit = labels[:, part] == columns
        small = jnp.exp(-jnp.abs(scores))
        signed = jnp.where(hit, -scores, scores)
        loss = loss + jnp.sum(jnp.maximum(signed, 0.0), axis=0, keepdims=True)
        product = small
        for _ in range(3):
            height = product.shape[0] // 2
            upper, lower = product[:height], product[height:]
            product = upper + lower + upper * lower
        loss = loss + jnp.sum(jnp.log1p(product), axis=0, keepdims=True)
        sigmoid = jnp.where(scores >= 0.0, 1.0, small) / (1.0 + small)
        slope = (sigmoid - hit.astype(f32)).astype(bf16)
        total = total + dot(slope, image_unit)
        upstream = contract_rows(slope, unit)
        along = jnp.sum(wide_unit * upstream, axis=-1, keepdims=True)
        image_parts[part, :] = (scale * inverse * (upstream - wide_unit * along)).astype(bf16)
    return total, loss


def score_kernel(params, base, image, text, labels, total_out, unit_out, image_parts, loss_out):
    unit = normalize(text[...])[0].astype(bf16)
    unit_out[...] = unit
    total = jnp.zeros(text.shape, f32)
    total, loss = score_rows(params, base, image, unit, labels, total, image_parts)
    total_out[...] = total
    loss_out[...] = loss


def rest_kernel(params, base, image, text, labels, total, unit, loss, text_parts, image_parts, halves):
    sums, more = score_rows(params, base, image, unit[...], labels, total[...], image_parts)
    text_parts[...] = project(text[...], params[0] * sums).astype(bf16)
    sums = jnp.sum(loss[...] + more, axis=1, keepdims=True)
    high = sums.astype(bf16).astype(f32)
    lane = lax.broadcasted_iota(jnp.int32, halves.shape, 1)
    row = lax.broadcasted_iota(jnp.int32, halves.shape, 0)
    values = jnp.where(lane == 0, high, jnp.where(lane == 1, sums - high, 0.0))
    halves[...] = jnp.where(row == base[1], values, 0.0).astype(bf16)


def like(array, dtype):
    return jax.ShapeDtypeStruct(array.shape, dtype)


def score_call(params, base, image, text, labels):
    return pl.pallas_call(
        score_kernel,
        out_shape=(
            like(text, f32),
            like(text, bf16),
            like(image, bf16),
            jax.ShapeDtypeStruct((1, CHUNK), f32),
        ),
        in_specs=[SMEM, SMEM, VMEM, VMEM, VMEM],
        out_specs=(VMEM, VMEM, VMEM, VMEM),
        compiler_params=pltpu.CompilerParams(vmem_limit_bytes=14 * 2**20),
        name="score",
    )(params, base, image, text, labels)


def rest_call(params, base, image, text, labels, total, unit, loss):
    return pl.pallas_call(
        rest_kernel,
        out_shape=(
            like(text, bf16),
            like(image, bf16),
            jax.ShapeDtypeStruct((8, text.shape[1]), bf16),
        ),
        in_specs=[SMEM, SMEM, VMEM, VMEM, VMEM, VMEM, VMEM, VMEM],
        out_specs=(VMEM, VMEM, VMEM),
        compiler_params=pltpu.CompilerParams(vmem_limit_bytes=14 * 2**20),
        name="score_rest",
    )(params, base, image, text, labels, total, unit, loss)


def packed(grad, acts, hidden, high, low):
    main = lax.dot_general(
        grad, acts[:256, :], (((0,), (1,)), ((), ())), preferred_element_type=f32
    )
    tail = dot(acts[256:, :], grad)
    row = lax.broadcasted_iota(jnp.int32, tail.shape, 0)
    tail = jnp.where(row == hidden - 256, high, jnp.where(row == hidden - 255, low, tail))
    width = grad.shape[1]
    height = width // 16
    for k in range(16):
        left, right = [
            pltpu.roll(half, (width - k * height) % width, 1)[:, :128] for half in (tail[:8], tail[8:])
        ]
        below = jnp.concatenate([left, right], axis=1)
        yield jnp.concatenate([main[k * height : (k + 1) * height], below], axis=0)


def finish_kernel(hidden, blocks, grad, value):
    total = jnp.zeros(blocks.shape[1:], f32)
    for k in range(blocks.shape[0]):
        total = total + blocks[k].astype(f32)
    height = grad.shape[0]
    grad[:, :256] = total[:height]
    tail = jnp.concatenate([total[height:, :128], total[height:, 128:]])
    grad[:, 256:] = tail.T[:height, : hidden - 256]
    value[...] = tail[hidden - 256 : hidden - 255, :1] + tail[hidden - 255 : hidden - 254, :1]


def finish_call(blocks, hidden):
    grad, value = pl.pallas_call(
        functools.partial(finish_kernel, hidden),
        out_shape=(
            jax.ShapeDtypeStruct((blocks.shape[1] - 8, hidden), f32),
            jax.ShapeDtypeStruct((1, 1), f32),
        ),
        in_specs=[VMEM],
        out_specs=(VMEM, VMEM),
        compiler_params=pltpu.CompilerParams(vmem_limit_bytes=6 * 2**20),
        name="finish",
    )(blocks)
    return grad.T, value


def weight_kernel(hidden, place, own, other, acts, proj, act_grad, blocks, back):
    y, c = place[0], place[1]
    rows, width = back.shape[-2:]
    loss = jnp.zeros((8, 128), f32)
    for d in range(4):
        at = lax.rem(y - d + 4, 4)
        for k in range(2):
            back[at, k, c] = own[d, k, :rows]
            back[at, k, 1 - c] = other[d, k, :rows]
            for part in (own, other):
                loss = loss + part[d, k, :, :128].astype(f32)[rows:]
    total = jnp.sum(jnp.sum(loss, axis=1, keepdims=True), axis=0, keepdims=True)
    high = total.astype(bf16).astype(f32)
    grad = back[...].reshape(-1, width)
    for k, block in enumerate(packed(grad, acts, hidden, high, total - high)):
        blocks[k] = block.astype(bf16)
    act_grad[...] = contract_cols(proj[...], grad).astype(bf16)


def weight_call(place, own, other, acts, proj, rows):
    hidden, width = proj.shape
    return pl.pallas_call(
        functools.partial(weight_kernel, hidden),
        out_shape=(
            jax.ShapeDtypeStruct((hidden, acts.shape[1]), bf16),
            jax.ShapeDtypeStruct((16, width // 16 + 8, 256), bf16),
        ),
        in_specs=[SMEM, VMEM, VMEM, VMEM, VMEM],
        out_specs=(VMEM, VMEM),
        scratch_shapes=[pltpu.VMEM((4, 2, 2, rows, width), bf16)],
        compiler_params=pltpu.CompilerParams(vmem_limit_bytes=16 * 2**20),
        name="image_weight",
    )(place, own, other, acts, proj)


def text_weight_kernel(hidden, place, back, acts, proj, act_grad, mine, theirs):
    blocks = list(packed(back[...], acts, hidden, 0.0, 0.0))
    for k in range(8):
        left, right = blocks[2 * k], blocks[2 * k + 1]
        mine[k // 2, k % 2] = jnp.where(place[1] == 0, left, right).astype(bf16)
        theirs[k // 2, k % 2] = jnp.where(place[1] == 0, right, left).astype(bf16)
    act_grad[...] = contract_cols(proj[...], back[...]).astype(bf16)


def text_weight_call(place, back, acts, proj):
    hidden, width = proj.shape
    shape = jax.ShapeDtypeStruct((4, 2, width // 16 + 8, 256), bf16)
    return pl.pallas_call(
        functools.partial(text_weight_kernel, hidden),
        out_shape=(jax.ShapeDtypeStruct((hidden, acts.shape[1]), bf16), shape, shape),
        in_specs=[SMEM, VMEM, VMEM, VMEM],
        out_specs=(VMEM, VMEM, VMEM),
        compiler_params=pltpu.CompilerParams(vmem_limit_bytes=16 * 2**20),
        name="text_weight",
    )(place, back, acts, proj)


def after(value, done):
    return lax.optimization_barrier((value, done))[0]


def on_device(
    image_hidden,
    image_acts,
    image_proj,
    text_hidden,
    text_acts,
    text_proj,
    positives,
    log_scale,
    bias,
):
    z, xl, y, xh, c = [lax.axis_index(name) for name in AXES]
    rows, width = image_hidden.shape
    hidden = text_proj.shape[0]
    total_rows = rows * 256
    scale = jnp.exp(log_scale[0])

    text_parts = dot(text_acts, text_proj).astype(bf16).reshape(16, rows, width)
    text_embed, copies = spread_call(exchange(text_parts, IMG), text_hidden, 8)

    image_acts = after(image_acts, text_parts)
    parts = dot(image_acts, image_proj).astype(bf16).reshape(4, 2, 2, rows, width)
    parts = (pick(parts, c, 2).astype(f32) + swap(pick(parts, 1 - c, 2), "c").astype(f32)).astype(bf16)
    total = pick(parts, y).astype(f32)
    for d in (1, 2, 3):
        total = total + shift(pick(parts, (y + d) % 4), "y", d).astype(f32)
    here = (jnp.arange(2, dtype=jnp.int32) == xh)[:, None, None]
    total = (total + jnp.where(here, image_hidden.astype(f32)[None], 0.0)).astype(bf16)
    image_row = jnp.stack(
        [
            total.astype(f32) + turn_x(total, 0, 1).astype(f32),
            turn_x(total, 1, 0).astype(f32) + turn_x(total, 1, 1).astype(f32),
        ]
    ).astype(bf16)

    positives_near = swap(positives, "xl")
    labels = pair(positives, positives_near, xl).reshape(2, 4, 2, 2, rows)
    n = jnp.arange(32, dtype=jnp.int32)
    core = jnp.where(n < 16, c, 1 - c)
    from_y = (y - n // 4 % 4) & 3
    order = (((xl ^ (n // 2 % 2)) * 4 + from_y) * 2 + n % 2) * 2 + core
    labels = jnp.take(labels.reshape(32, rows), order, axis=0).reshape(1, -1)
    base = jnp.stack([((y * 2 + xh) * 2 + c) * 512 + xl * rows, xl * 2 + xh]).astype(jnp.int32)
    params = jnp.stack([scale, bias[0]])
    text_block = exchange(after(copies, (image_row, labels, params, base)), "z").reshape(-1, width)
    own_block = gather_y(after(image_row, text_embed)).reshape(-1, width)
    near_block = swap(after(own_block, text_block), "c")

    half = 16 * rows
    text_total, text_unit, mine, losses = score_call(
        params, base, own_block, text_block, labels[:, :half]
    )
    text_parts, theirs, halves = rest_call(
        params, base, near_block, text_block, labels[:, half:], text_total, text_unit, losses
    )
    text_grad, copies = spread_call(
        exchange(text_parts.reshape(8, rows, width), "z"), jnp.zeros((rows, width), bf16), 16
    )
    theirs = swap(theirs, "c")
    slab = (mine.astype(f32) + theirs.astype(f32)).astype(bf16)
    image_row = sum_y(slab.reshape(4, 4, rows, width)).reshape(2, 2, rows, width)

    image_row = after(image_row, text_grad)
    halves = jnp.broadcast_to(halves, (2, 2) + halves.shape)
    image_row = jnp.concatenate([image_row, halves], axis=2)
    near = image_row[0].astype(f32) + turn_x(image_row[0], 0, 1).astype(f32)
    near = near + turn_x(image_row[1], 1, 0).astype(f32) + turn_x(image_row[1], 1, 1).astype(f32)
    near = near.astype(bf16)
    image_grad = pick(near, xh)[:rows]
    ring = gather_y(near)
    place = jnp.stack([y, c]).astype(jnp.int32)
    wide = ((0, 272 - hidden), (0, 0))
    image_act_grad, blocks = weight_call(
        place, ring, swap(ring, "c"), jnp.pad(image_acts.T, wide), image_proj, rows
    )
    found = exchange(blocks, IMG)

    text_back = exchange(after(copies, image_row), IMG).reshape(-1, width)
    text_back = after(text_back, blocks)
    text_act_grad, mine, theirs = text_weight_call(
        place, text_back, jnp.pad(text_acts.T, wide), text_proj
    )
    parts = (mine.astype(f32) + swap(theirs, "c").astype(f32)).astype(bf16)
    total = pick(parts, y).astype(f32)
    for d in (1, 2, 3):
        total = total + shift(pick(parts, (y + d) % 4), "y", d).astype(f32)
    total = total.astype(bf16)
    last = jnp.stack([pick(total, xh), swap(pick(total, 1 - xh), "xh")])

    text_proj_grad = finish_call(last, hidden)[0]
    image_proj_grad, total_loss = finish_call(after(found, last), hidden)
    loss = jnp.reshape(0.25 * total_loss / total_rows, (1,))
    return (
        loss,
        image_grad,
        text_grad,
        image_act_grad.T,
        text_act_grad.T,
        image_proj_grad,
        text_proj_grad,
    )


def solution(mesh):
    fine = Mesh(mesh.devices.reshape(SIZES), AXES)
    return jax.shard_map(
        on_device,
        mesh=fine,
        in_specs=(
            P(IMG + TXT, None),
            P(IMG, TXT),
            P(TXT, None),
            P(TXT + IMG, None),
            P(TXT, IMG),
            P(IMG, None),
            P(IMG),
            P(),
            P(),
        ),
        out_specs=(
            P(),
            P(IMG + TXT, None),
            P(TXT + IMG, None),
            P(IMG, TXT),
            P(TXT, IMG),
            P(TXT, IMG),
            P(IMG, TXT),
        ),
        check_vma=False,
    )
```

```python
import functools

import jax
import jax.numpy as jnp
from jax import lax
from jax.experimental import pallas as pl
from jax.experimental.pallas import tpu as pltpu
from jax.sharding import Mesh, PartitionSpec as P

AXES = ("z", "xl", "y", "xh", "c")
SIZES = (8, 2, 4, 2, 2)
IMG = ("z", "xl")
TXT = ("y", "xh", "c")
PLANE = ("xl", "y", "xh")
SWAP = [(0, 1), (1, 0)]
f32 = jnp.float32
bf16 = jnp.bfloat16


def normalize(embed):
    values = embed.astype(f32)
    inverse = lax.rsqrt(jnp.sum(values * values, axis=-1, keepdims=True) + 1e-06)
    return (values * inverse, inverse)


def project(embed, upstream):
    unit, inverse = normalize(embed)
    return inverse * (upstream - unit * jnp.sum(unit * upstream, axis=-1, keepdims=True))


def dot(left, right):
    return jnp.dot(left, right, preferred_element_type=f32)


def contract_rows(left, right):
    return lax.dot_general(left, right, (((0,), (0,)), ((), ())), preferred_element_type=f32)


def contract_cols(left, right):
    return lax.dot_general(left, right, (((1,), (1,)), ((), ())), preferred_element_type=f32)


def pick(blocks, index, axis=0):
    return lax.dynamic_index_in_dim(blocks, index, axis, keepdims=False)


def swap(block, axis):
    return lax.ppermute(block, axis, SWAP)


def pair(mine, other, index):
    return jnp.where(index == 0, jnp.stack([mine, other]), jnp.stack([other, mine]))


def shift(block, axis, step, count=4):
    return lax.ppermute(block, axis, [(i, (i + step) % count) for i in range(count)])


def gather_y(block):
    return jnp.stack([block] + [shift(block, "y", d) for d in (1, 2, 3)])


def sum_y(blocks):
    total = blocks[0].astype(f32)
    for d in (1, 2, 3):
        total = total + shift(blocks[d], "y", 4 - d).astype(f32)
    return total.astype(bf16)


def turn_x(block, a, b):
    return lax.ppermute(block, ("xl", "xh"), [(i, i ^ (2 * a + b)) for i in range(4)])


def exchange(blocks, axis):
    return lax.all_to_all(blocks, axis, 0, 0)


def spread_kernel(parts, base, row, copies):
    total = base[...].astype(f32)
    for k in range(parts.shape[0]):
        total = total + parts[k].astype(f32)
    total = total.astype(bf16)
    row[...] = total
    for k in range(copies.shape[0]):
        copies[k] = total


def spread_call(parts, base, count):
    return pl.pallas_call(
        spread_kernel,
        out_shape=(
            jax.ShapeDtypeStruct(base.shape, bf16),
            jax.ShapeDtypeStruct((count,) + base.shape, bf16),
        ),
        in_specs=[VMEM, VMEM],
        out_specs=(VMEM, VMEM),
        compiler_params=pltpu.CompilerParams(vmem_limit_bytes=8 * 2**20),
        name="spread",
    )(parts, base)


CHUNK = 512
VMEM = pl.BlockSpec(memory_space=pltpu.VMEM)
SMEM = pl.BlockSpec(memory_space=pltpu.SMEM)


def score_rows(params, base, image, unit, labels, total, image_parts):
    scale, bias = params[0], params[1]
    index = lax.broadcasted_iota(jnp.int32, (unit.shape[0], 1), 0)
    columns = base[0] + index + (index & -32)
    loss = jnp.zeros((1, CHUNK), f32)
    for start in range(0, image.shape[0], CHUNK):
        part = pl.ds(start, CHUNK)
        wide_unit, inverse = normalize(image[part, :])
        image_unit = wide_unit.astype(bf16)
        scores = scale * contract_cols(unit, image_unit) + bias
        hit = labels[:, part] == columns
        small = jnp.exp(-jnp.abs(scores))
        signed = jnp.where(hit, -scores, scores)
        loss = loss + jnp.sum(jnp.maximum(signed, 0.0), axis=0, keepdims=True)
        product = small
        for _ in range(3):
            height = product.shape[0] // 2
            upper, lower = product[:height], product[height:]
            product = upper + lower + upper * lower
        loss = loss + jnp.sum(jnp.log1p(product), axis=0, keepdims=True)
        sigmoid = jnp.where(scores >= 0.0, 1.0, small) / (1.0 + small)
        slope = (sigmoid - hit.astype(f32)).astype(bf16)
        total = total + dot(slope, image_unit)
        upstream = contract_rows(slope, unit)
        along = jnp.sum(wide_unit * upstream, axis=-1, keepdims=True)
        image_parts[part, :] = (scale * inverse * (upstream - wide_unit * along)).astype(bf16)
    return total, loss


def score_kernel(params, base, image, text, labels, total_out, unit_out, image_parts, loss_out):
    unit = normalize(text[...])[0].astype(bf16)
    unit_out[...] = unit
    total = jnp.zeros(text.shape, f32)
    total, loss = score_rows(params, base, image, unit, labels, total, image_parts)
    total_out[...] = total
    loss_out[...] = loss


def rest_kernel(params, base, image, text, labels, total, unit, loss, text_parts, image_parts, halves):
    sums, more = score_rows(params, base, image, unit[...], labels, total[...], image_parts)
    text_parts[...] = project(text[...], params[0] * sums).astype(bf16)
    sums = jnp.sum(loss[...] + more, axis=1, keepdims=True)
    high = sums.astype(bf16).astype(f32)
    lane = lax.broadcasted_iota(jnp.int32, halves.shape, 1)
    row = lax.broadcasted_iota(jnp.int32, halves.shape, 0)
    values = jnp.where(lane == 0, high, jnp.where(lane == 1, sums - high, 0.0))
    halves[...] = jnp.where(row == base[1], values, 0.0).astype(bf16)


def like(array, dtype):
    return jax.ShapeDtypeStruct(array.shape, dtype)


def score_call(params, base, image, text, labels):
    return pl.pallas_call(
        score_kernel,
        out_shape=(
            like(text, f32),
            like(text, bf16),
            like(image, bf16),
            jax.ShapeDtypeStruct((1, CHUNK), f32),
        ),
        in_specs=[SMEM, SMEM, VMEM, VMEM, VMEM],
        out_specs=(VMEM, VMEM, VMEM, VMEM),
        compiler_params=pltpu.CompilerParams(vmem_limit_bytes=14 * 2**20),
        name="score",
    )(params, base, image, text, labels)


def rest_call(params, base, image, text, labels, total, unit, loss):
    return pl.pallas_call(
        rest_kernel,
        out_shape=(
            like(text, bf16),
            like(image, bf16),
            jax.ShapeDtypeStruct((8, text.shape[1]), bf16),
        ),
        in_specs=[SMEM, SMEM, VMEM, VMEM, VMEM, VMEM, VMEM, VMEM],
        out_specs=(VMEM, VMEM, VMEM),
        compiler_params=pltpu.CompilerParams(vmem_limit_bytes=14 * 2**20),
        name="score_rest",
    )(params, base, image, text, labels, total, unit, loss)


def packed(grad, acts, hidden, high, low):
    main = lax.dot_general(
        grad, acts[:256, :], (((0,), (1,)), ((), ())), preferred_element_type=f32
    )
    tail = dot(acts[256:, :], grad)
    row = lax.broadcasted_iota(jnp.int32, tail.shape, 0)
    tail = jnp.where(row == hidden - 256, high, jnp.where(row == hidden - 255, low, tail))
    width = grad.shape[1]
    height = width // 16
    for k in range(16):
        left, right = [
            pltpu.roll(half, (width - k * height) % width, 1)[:, :128] for half in (tail[:8], tail[8:])
        ]
        below = jnp.concatenate([left, right], axis=1)
        yield jnp.concatenate([main[k * height : (k + 1) * height], below], axis=0)


def finish_kernel(hidden, blocks, grad, value):
    total = jnp.zeros(blocks.shape[1:], f32)
    for k in range(blocks.shape[0]):
        total = total + blocks[k].astype(f32)
    height = grad.shape[0]
    grad[:, :256] = total[:height]
    tail = jnp.concatenate([total[height:, :128], total[height:, 128:]])
    grad[:, 256:] = tail.T[:height, : hidden - 256]
    value[...] = tail[hidden - 256 : hidden - 255, :1] + tail[hidden - 255 : hidden - 254, :1]


def finish_call(blocks, hidden):
    grad, value = pl.pallas_call(
        functools.partial(finish_kernel, hidden),
        out_shape=(
            jax.ShapeDtypeStruct((blocks.shape[1] - 8, hidden), f32),
            jax.ShapeDtypeStruct((1, 1), f32),
        ),
        in_specs=[VMEM],
        out_specs=(VMEM, VMEM),
        compiler_params=pltpu.CompilerParams(vmem_limit_bytes=6 * 2**20),
        name="finish",
    )(blocks)
    return grad.T, value


def weight_kernel(hidden, place, own, other, acts, proj, act_grad, blocks, back):
    y, c = place[0], place[1]
    rows, width = back.shape[-2:]
    loss = jnp.zeros((8, 128), f32)
    for d in range(4):
        at = lax.rem(y - d + 4, 4)
        for k in range(2):
            back[at, k, c] = own[d, k, :rows]
            back[at, k, 1 - c] = other[d, k, :rows]
            for part in (own, other):
                loss = loss + part[d, k, :, :128].astype(f32)[rows:]
    total = jnp.sum(jnp.sum(loss, axis=1, keepdims=True), axis=0, keepdims=True)
    high = total.astype(bf16).astype(f32)
    grad = back[...].reshape(-1, width)
    for k, block in enumerate(packed(grad, acts, hidden, high, total - high)):
        blocks[k] = block.astype(bf16)
    act_grad[...] = contract_cols(proj[...], grad).astype(bf16)


def weight_call(place, own, other, acts, proj, rows):
    hidden, width = proj.shape
    return pl.pallas_call(
        functools.partial(weight_kernel, hidden),
        out_shape=(
            jax.ShapeDtypeStruct((hidden, acts.shape[1]), bf16),
            jax.ShapeDtypeStruct((16, width // 16 + 8, 256), bf16),
        ),
        in_specs=[SMEM, VMEM, VMEM, VMEM, VMEM],
        out_specs=(VMEM, VMEM),
        scratch_shapes=[pltpu.VMEM((4, 2, 2, rows, width), bf16)],
        compiler_params=pltpu.CompilerParams(vmem_limit_bytes=16 * 2**20),
        name="image_weight",
    )(place, own, other, acts, proj)


def text_weight_kernel(hidden, place, back, acts, proj, act_grad, mine, theirs):
    blocks = list(packed(back[...], acts, hidden, 0.0, 0.0))
    for k in range(8):
        left, right = blocks[2 * k], blocks[2 * k + 1]
        mine[k // 2, k % 2] = jnp.where(place[1] == 0, left, right).astype(bf16)
        theirs[k // 2, k % 2] = jnp.where(place[1] == 0, right, left).astype(bf16)
    act_grad[...] = contract_cols(proj[...], back[...]).astype(bf16)


def text_weight_call(place, back, acts, proj):
    hidden, width = proj.shape
    shape = jax.ShapeDtypeStruct((4, 2, width // 16 + 8, 256), bf16)
    return pl.pallas_call(
        functools.partial(text_weight_kernel, hidden),
        out_shape=(jax.ShapeDtypeStruct((hidden, acts.shape[1]), bf16), shape, shape),
        in_specs=[SMEM, VMEM, VMEM, VMEM],
        out_specs=(VMEM, VMEM, VMEM),
        compiler_params=pltpu.CompilerParams(vmem_limit_bytes=16 * 2**20),
        name="text_weight",
    )(place, back, acts, proj)


def after(value, done):
    return lax.optimization_barrier((value, done))[0]


def on_device(
    image_hidden,
    image_acts,
    image_proj,
    text_hidden,
    text_acts,
    text_proj,
    positives,
    log_scale,
    bias,
):
    z, xl, y, xh, c = [lax.axis_index(name) for name in AXES]
    rows, width = image_hidden.shape
    hidden = text_proj.shape[0]
    total_rows = rows * 256
    scale = jnp.exp(log_scale[0])

    text_parts = dot(text_acts, text_proj).astype(bf16).reshape(16, rows, width)
    text_embed, copies = spread_call(exchange(text_parts, IMG), text_hidden, 8)

    image_acts = after(image_acts, text_parts)
    parts = dot(image_acts, image_proj).astype(bf16).reshape(4, 2, 2, rows, width)
    parts = (pick(parts, c, 2).astype(f32) + swap(pick(parts, 1 - c, 2), "c").astype(f32)).astype(bf16)
    total = pick(parts, y).astype(f32)
    for d in (1, 2, 3):
        total = total + shift(pick(parts, (y + d) % 4), "y", d).astype(f32)
    here = (jnp.arange(2, dtype=jnp.int32) == xh)[:, None, None]
    total = (total + jnp.where(here, image_hidden.astype(f32)[None], 0.0)).astype(bf16)
    image_row = jnp.stack(
        [
            total.astype(f32) + turn_x(total, 0, 1).astype(f32),
            turn_x(total, 1, 0).astype(f32) + turn_x(total, 1, 1).astype(f32),
        ]
    ).astype(bf16)

    positives_near = swap(positives, "xl")
    labels = pair(positives, positives_near, xl).reshape(2, 4, 2, 2, rows)
    n = jnp.arange(32, dtype=jnp.int32)
    core = jnp.where(n < 16, c, 1 - c)
    from_y = (y - n // 4 % 4) & 3
    order = (((xl ^ (n // 2 % 2)) * 4 + from_y) * 2 + n % 2) * 2 + core
    labels = jnp.take(labels.reshape(32, rows), order, axis=0).reshape(1, -1)
    base = jnp.stack([((y * 2 + xh) * 2 + c) * 512 + xl * rows, xl * 2 + xh]).astype(jnp.int32)
    params = jnp.stack([scale, bias[0]])
    text_block = exchange(after(copies, (image_row, labels, params, base)), "z").reshape(-1, width)
    own_block = gather_y(after(image_row, text_embed)).reshape(-1, width)
    near_block = swap(after(own_block, text_block), "c")

    half = 16 * rows
    text_total, text_unit, mine, losses = score_call(
        params, base, own_block, text_block, labels[:, :half]
    )
    text_parts, theirs, halves = rest_call(
        params, base, near_block, text_block, labels[:, half:], text_total, text_unit, losses
    )
    text_grad, copies = spread_call(
        exchange(text_parts.reshape(8, rows, width), "z"), jnp.zeros((rows, width), bf16), 16
    )
    theirs = swap(theirs, "c")
    slab = (mine.astype(f32) + theirs.astype(f32)).astype(bf16)
    image_row = sum_y(slab.reshape(4, 4, rows, width)).reshape(2, 2, rows, width)

    image_row = after(image_row, text_grad)
    halves = jnp.broadcast_to(halves, (2, 2) + halves.shape)
    image_row = jnp.concatenate([image_row, halves], axis=2)
    near = image_row[0].astype(f32) + turn_x(image_row[0], 0, 1).astype(f32)
    near = near + turn_x(image_row[1], 1, 0).astype(f32) + turn_x(image_row[1], 1, 1).astype(f32)
    near = near.astype(bf16)
    image_grad = pick(near, xh)[:rows]
    ring = gather_y(near)
    place = jnp.stack([y, c]).astype(jnp.int32)
    wide = ((0, 272 - hidden), (0, 0))
    image_act_grad, blocks = weight_call(
        place, ring, swap(ring, "c"), jnp.pad(image_acts.T, wide), image_proj, rows
    )
    found = exchange(blocks, IMG)

    text_back = exchange(copies, IMG).reshape(-1, width)
    text_back = after(text_back, blocks)
    text_act_grad, mine, theirs = text_weight_call(
        place, text_back, jnp.pad(text_acts.T, wide), text_proj
    )
    parts = (mine.astype(f32) + swap(theirs, "c").astype(f32)).astype(bf16)
    total = pick(parts, y).astype(f32)
    for d in (1, 2, 3):
        total = total + shift(pick(parts, (y + d) % 4), "y", d).astype(f32)
    total = total.astype(bf16)
    last = jnp.stack([pick(total, xh), swap(pick(total, 1 - xh), "xh")])

    text_proj_grad = finish_call(last, hidden)[0]
    image_proj_grad, total_loss = finish_call(after(found, last), hidden)
    loss = jnp.reshape(0.25 * total_loss / total_rows, (1,))
    return (
        loss,
        image_grad,
        text_grad,
        image_act_grad.T,
        text_act_grad.T,
        image_proj_grad,
        text_proj_grad,
    )


def solution(mesh):
    fine = Mesh(mesh.devices.reshape(SIZES), AXES)
    return jax.shard_map(
        on_device,
        mesh=fine,
        in_specs=(
            P(IMG + TXT, None),
            P(IMG, TXT),
            P(TXT, None),
            P(TXT + IMG, None),
            P(TXT, IMG),
            P(IMG, None),
            P(IMG),
            P(),
            P(),
        ),
        out_specs=(
            P(),
            P(IMG + TXT, None),
            P(TXT + IMG, None),
            P(IMG, TXT),
            P(TXT, IMG),
            P(TXT, IMG),
            P(IMG, TXT),
        ),
        check_vma=False,
    )
```
